32 devices in a mesh: parts: 1, dp: 4 (over x, core), expert: 8 (over z, y).
Axes of the slice: x: 2, y: 2, z: 4, core: 2. Of those that a mesh axis runs over, the one named last changes fastest.
Arguments:
- hidden: bfloat16 [64, 2048], P(('parts', 'dp')), may hold values from -6 to 6
- states: float32 [64, 8, 128, 128], P(('parts', 'dp'), 'expert'), may hold values from -0.6 to 0.6
- migration: int32 [16, 4], P('parts'), may hold values from 0 to 15, as said below
- routes: int32 [64, 10], P('parts'), may hold values from 0 to 31, all different within a row; in each aligned block of 64 rows (0 to 63, 64 to 127, ...) at most 40 rows name the same one
- w_qkvz: bfloat16 [2048, 3072], P('dp', 'expert'), may hold values from -0.125 to 0.125
- w_ba: bfloat16 [2048, 16], P('dp', 'expert'), may hold values from -0.125 to 0.125
- a_log: float32 [8], P('expert'), may hold values from -2.5 to 1
- dt_bias: float32 [8], P('expert'), may hold values from -3 to 1
- attn_gain: float32 [2048], replicated, may hold values from 0.1 to 1.9
- head_gain: float32 [128], replicated, may hold values from 0.1 to 1.9
- w_out: bfloat16 [1024, 2048], P('expert'), may hold values from -0.1875 to 0.1875
- moe_gain: float32 [2048], replicated, may hold values from 0.1 to 1.9
- w_router: bfloat16 [2048, 32], P(None, ('dp', 'expert')), may hold values from -0.125 to 0.125
- w_gate_up: bfloat16 [32, 2048, 512], P(('dp', 'expert')), may hold values from -0.125 to 0.125
- w_down: bfloat16 [32, 256, 2048], P(('dp', 'expert')), may hold values from -0.375 to 0.375
Outputs:
- mixed: bfloat16 [64, 2048], P(('parts', 'dp'), 'expert')
The draws below stay inside these ranges and needn't reach their ends.
Inputs may be any that keep to these rules, and one draw needn't show every extreme that they name: `migration`: row g * 4 + j holds group g's j-th leaving row. Each group sends 4 rows from distinct slots to 4 different groups (itself possibly), and receives exactly one row from each of 4 groups, into distinct slots. Group numbers are below 4, slots below 16. `routes`: each row names 10 different experts; no expert is named by more than 40 rows.
All inputs are finite; a program needn't handle non-finite values.
Results may differ from the reference program's by a relative error of at most 0.0064.
Values may be sent and summed in bfloat16 or wider, within the bound.
No kernel may reach another device: no remote copies, remote signals or barrier semaphores. Data moves between devices by JAX's collectives and lax.ppermute only.
A program may use at most 64 MiB of HBM per device.

```python
import math
import jax
import jax.numpy as jnp
import numpy as np
from jax import lax

D = 2048
DK = 128
DV = 128
MOE_FF = 256
TOPK = 10
ROWS_GRP = 16
MIG_GRP = 4
HV = 8
EXPERTS = 32
ROWS = 64
MIG = 16
CAPE = 40


def slot_order(sub_key):
    order = jax.random.permutation(sub_key, ROWS_GRP).astype(jnp.int32)
    where_last = jnp.argmax(order == ROWS_GRP - 1).astype(jnp.int32)
    order = order.at[where_last].set(order[0])
    return order.at[0].set(ROWS_GRP - 1)


def draw_migration(key, part):
    key = jax.random.fold_in(key, 17)
    keys_all = jax.random.split(key, 5)
    group_count = MIG // MIG_GRP
    sigma_perm = jax.random.permutation(keys_all[0], group_count).astype(jnp.int32)
    shuffle_perm = jax.random.permutation(keys_all[1], group_count).astype(jnp.int32)
    offsets = jax.random.permutation(keys_all[2], group_count)[:MIG_GRP].astype(jnp.int32)
    source_group = jnp.repeat(jnp.arange(group_count, dtype=jnp.int32), MIG_GRP)
    turn_index = jnp.tile(jnp.arange(MIG_GRP, dtype=jnp.int32), group_count)
    target_group = sigma_perm[(shuffle_perm[source_group] + offsets[turn_index]) % group_count]
    source_table = jax.vmap(slot_order)(jax.random.split(keys_all[3], group_count))[:, :MIG_GRP]
    target_table = jax.vmap(lambda sub_key: jax.random.permutation(sub_key, ROWS_GRP))(jax.random.split(keys_all[4], group_count))[:, :MIG_GRP]
    source_slot = source_table.reshape(-1).astype(jnp.int32)
    target_slot = target_table[target_group, turn_index].astype(jnp.int32)
    return jnp.stack([source_group, source_slot, target_group, target_slot], axis=1).astype(jnp.int32)


def steps_of(stream_key, shape, cuts, smallest, high):
    factor_of, own = 1.0, jax.random.fold_in(stream_key, 6)
    for position, parts in cuts:
        steps = jnp.exp(jax.random.uniform(jax.random.fold_in(own, position), (parts,), jnp.float32, smallest / len(cuts), high / len(cuts)))
        factor_of = factor_of * jnp.repeat(steps, shape[position] // parts).reshape([-1 if axis == position else 1 for axis in range(len(shape))])
    return factor_of


def assign_block(stream_key, own, number, rows, amount, top, most, lean):
    ranking = jax.random.permutation(stream_key, amount)
    crowded, common = load_shares(amount, rows * top, most, lean, True), load_shares(amount, rows * top, most, lean, False)
    places = jnp.arange(amount)

    def named(tallies, turn):
        used = int((tallies > 0).sum())
        fixed = max(1, used // 4)
        moved = fixed + (places - fixed + turn * (used - fixed)) % max(1, amount - fixed)
        return jnp.zeros((amount,), jnp.int32).at[ranking[jnp.where(places < fixed, places, moved)]].set(jnp.asarray(tallies, jnp.int32))

    tallies = jnp.where(number % 4 == 0, named(crowded, number // 4), named(common, number - number // 4 - 1))
    mixed = jax.random.permutation(jax.random.fold_in(own, 3), amount)
    donor, receiver = mixed[0:amount // 2 * 2:2], mixed[1:amount // 2 * 2:2]
    slack = jnp.minimum(tallies[donor] - 1, most - tallies[receiver]) // 2
    slack = jnp.where((donor == ranking[0]) | (receiver == ranking[0]) | (tallies[receiver] == 0), 0, jnp.maximum(slack, 0))
    moved = jax.random.randint(jax.random.fold_in(own, 4), (amount // 2,), 0, 1 << 20) % (slack + 1)
    tallies = tallies.at[donor].add(-moved).at[receiver].add(moved)
    items = jnp.searchsorted(jnp.cumsum(tallies), jnp.arange(rows * top), side="right").astype(jnp.int32)
    grid = items.reshape(top, rows).T
    grid = grid[jax.random.permutation(jax.random.fold_in(own, 1), rows)]
    turn = jax.random.randint(jax.random.fold_in(own, 2), (rows, 1), 0, top)
    return jnp.take_along_axis(grid, (jnp.arange(top)[None, :] + turn) % top, axis=1)


def load_shares(number_of, total, most, skew, full):
    loads = [(1 << 20) // math.isqrt(rank ** skew) + 1 for rank in range(1, number_of + 1)]
    largest = most if full else min(most, max(-(-total // number_of), total * loads[0] // sum(loads)))
    least = 1 if total - largest >= number_of - 1 else 0
    counts, rest = [largest] + [least] * (number_of - 1), total - largest - least * (number_of - 1)
    while rest > 0:
        free = [i for i in range(1, number_of) if counts[i] < largest] or [i for i in range(1, number_of) if counts[i] < most]
        whole, left = sum([loads[i] for i in free]), rest
        for i in free:
            extra = min(most - counts[i], max(1, left * loads[i] // whole), rest)
            counts[i] = counts[i] + extra
            rest = rest - extra
    return np.array(counts)


def noise(stream_key, extent, deviation, bound, cuts=(), kind=jnp.bfloat16):
    factor_of = steps_of(stream_key, extent, cuts, -0.22, 0.18) if cuts else 1.0
    drawn = jax.random.normal(stream_key, extent, jnp.float32) * deviation * factor_of
    return jnp.minimum(jnp.maximum(drawn, -bound), bound).astype(kind)


def setup_inputs(seed: int = 0, part: int = 0) -> dict:
    streams_of = jax.random.split(jax.random.key(seed), 16)
    own_keys = jax.random.split(jax.random.fold_in(streams_of[15], part), 16)
    hidden = noise(own_keys[0], (ROWS, D), 1.0, 6.0, ((0, 4),))
    states = noise(own_keys[1], (ROWS, HV, DK, DV), 0.1, 0.6, ((0, 4), (1, 8)), jnp.float32)
    migration = draw_migration(jax.random.fold_in(jax.random.fold_in(streams_of[15], part), 71), part)
    routes_keys = jax.random.split(jax.random.fold_in(own_keys[3], 1), ROWS // ROWS)
    routes_turns = jax.random.permutation(jax.random.fold_in(own_keys[3], 3), ROWS // ROWS)
    routes = jax.vmap(lambda own, number: assign_block(jax.random.fold_in(own_keys[3], 2), own, number, ROWS, EXPERTS, TOPK, CAPE, 1))(routes_keys, routes_turns).reshape((ROWS, TOPK))
    w_qkvz = noise(streams_of[4], (D, HV * (DK + 2 * DV)), D ** -0.5, 0.125, ((0, 4), (1, 8)))
    w_ba = noise(streams_of[5], (D, 2 * HV), D ** -0.5, 0.125, ((0, 4), (1, 8)))
    a_log = jnp.clip(-2.5 + 3.5 * jax.random.uniform(streams_of[6], (HV,), jnp.float32) ** steps_of(streams_of[6], (HV,), ((0, 8),), -0.2, 0.2), -2.5, 1.0)
    dt_bias = jnp.clip(-3.0 + 4.0 * jax.random.uniform(streams_of[7], (HV,), jnp.float32) ** steps_of(streams_of[7], (HV,), ((0, 8),), -0.2, 0.2), -3.0, 1.0)
    attn_gain = jnp.clip(1.0 + 0.18 * jax.random.normal(streams_of[8], (D,), jnp.float32), 0.1, 1.9)
    head_gain = jnp.clip(1.0 + 0.18 * jax.random.normal(streams_of[9], (DV,), jnp.float32), 0.1, 1.9)
    w_out = noise(streams_of[10], (HV * DV, D), (HV * DV) ** -0.5, 0.1875, ((0, 8),))
    moe_gain = jnp.clip(1.0 + 0.18 * jax.random.normal(streams_of[11], (D,), jnp.float32), 0.1, 1.9)
    w_router = noise(streams_of[12], (D, EXPERTS), D ** -0.5, 0.125, ((1, 32),))
    w_gate_up = noise(streams_of[13], (EXPERTS, D, 2 * MOE_FF), D ** -0.5, 0.125, ((0, 32),))
    w_down = noise(streams_of[14], (EXPERTS, MOE_FF, D), MOE_FF ** -0.5, 0.375, ((0, 32),))
    return dict(hidden=hidden, states=states, migration=migration, routes=routes, w_qkvz=w_qkvz, w_ba=w_ba, a_log=a_log, dt_bias=dt_bias, attn_gain=attn_gain, head_gain=head_gain, w_out=w_out, moe_gain=moe_gain, w_router=w_router, w_gate_up=w_gate_up, w_down=w_down)


EPS = 1e-06

def norm_rows(values, gain):
    values = values.astype(jnp.float32)
    return values * lax.rsqrt(lax.optimization_barrier(jnp.mean(values * values, axis=-1, keepdims=True)) + EPS) * gain

def unit_rows(values):
    return values * lax.rsqrt(lax.optimization_barrier(jnp.sum(values * values, axis=-1, keepdims=True)) + EPS)

def reference(hidden, states, migration, routes, w_qkvz, w_ba, a_log, dt_bias, attn_gain, head_gain, w_out, moe_gain, w_router, w_gate_up, w_down):
    source_rows = (migration[:, 0] * ROWS_GRP + migration[:, 1]).astype(jnp.int32)
    target_rows = (migration[:, 2] * ROWS_GRP + migration[:, 3]).astype(jnp.int32)
    carried = states.at[target_rows].set(states[source_rows])
    normed_in = norm_rows(hidden, attn_gain).astype(jnp.bfloat16)
    projected = jnp.dot(normed_in, w_qkvz, preferred_element_type=jnp.float32).astype(jnp.bfloat16)
    projected = projected.reshape(ROWS, HV, DK + 2 * DV)
    mix_values = jnp.dot(normed_in, w_ba, preferred_element_type=jnp.float32).astype(jnp.bfloat16)
    mix_values = mix_values.reshape(ROWS, HV, 2).astype(jnp.float32)
    half_width = DK // 2
    query_half = projected[:, :, :half_width].astype(jnp.float32).reshape(ROWS, HV // 2, DK)
    key_half = projected[:, :, half_width:DK].astype(jnp.float32).reshape(ROWS, HV // 2, DK)
    queries = unit_rows(jnp.repeat(query_half, 2, axis=1)) * DK ** (-0.5)
    keys_unit = unit_rows(jnp.repeat(key_half, 2, axis=1))
    values = projected[:, :, DK:DK + DV].astype(jnp.float32)
    out_gate = projected[:, :, DK + DV:].astype(jnp.float32)
    beta_gate = jax.nn.sigmoid(mix_values[:, :, 0])
    decay_rate = jnp.exp(-jnp.exp(a_log)[None, :] * jax.nn.softplus(mix_values[:, :, 1] + dt_bias[None, :]))
    updated = carried * decay_rate[:, :, None, None]
    recalled = jnp.einsum('rhk,rhkv->rhv', keys_unit, updated, precision=lax.Precision.HIGHEST)
    correction = (values - recalled) * beta_gate[:, :, None]
    updated = updated + keys_unit[:, :, :, None] * correction[:, :, None, :]
    readout = jnp.einsum('rhk,rhkv->rhv', queries, updated, precision=lax.Precision.HIGHEST)
    gated = (norm_rows(readout, head_gain) * jax.nn.silu(out_gate)).astype(jnp.bfloat16)
    attention = jnp.dot(gated.reshape(ROWS, HV * DV), w_out, preferred_element_type=jnp.float32)
    residual = hidden.astype(jnp.float32) + attention
    normed_moe = norm_rows(residual, moe_gain).astype(jnp.bfloat16)
    logits = jnp.dot(normed_moe, w_router, preferred_element_type=jnp.float32)
    shares = jnp.exp(jnp.take_along_axis(logits, routes, axis=1))
    denominator = lax.optimization_barrier(jnp.sum(shares, axis=1))

    def expert_step(numerator, inputs):
        gate_up, down_proj, expert_index = inputs
        matches = routes == expert_index
        hit_rows = jnp.any(matches, axis=1)
        coefficient = lax.optimization_barrier(jnp.sum(jnp.where(matches, shares, jnp.zeros_like(shares)), axis=1))
        row_index = jnp.nonzero(hit_rows, size=CAPE, fill_value=0)[0].astype(jnp.int32)
        picked = normed_moe[row_index]
        gate_up_out = jnp.dot(picked, gate_up, preferred_element_type=jnp.float32)
        hidden_act = (jax.nn.silu(gate_up_out[:, :MOE_FF]) * gate_up_out[:, MOE_FF:]).astype(jnp.bfloat16)
        output = jnp.dot(hidden_act, down_proj, preferred_element_type=jnp.float32)
        live = jnp.arange(CAPE, dtype=jnp.int32) < jnp.sum(hit_rows.astype(jnp.int32))
        weight = jnp.where(live, coefficient[row_index], jnp.zeros_like(coefficient[row_index]))
        numerator = numerator.at[row_index].add(weight[:, None] * output)
        return (numerator, None)
    start_sum = jnp.zeros((ROWS, D), jnp.float32)
    numerator, unused = lax.scan(expert_step, start_sum, (w_gate_up, w_down, jnp.arange(EXPERTS, dtype=jnp.int32)))
    return (residual + numerator / denominator[:, None]).astype(jnp.bfloat16)
```

```python
import jax
import jax.numpy as jnp
from jax import lax
from jax.sharding import PartitionSpec as P

DK = 128
DV = 128
MOE_FF = 256

EPS = 1e-06
BF = jnp.bfloat16
F32 = jnp.float32


def swap_with(value, axis, offset):
    pairs = [(source, source ^ offset) for source in range(lax.axis_size(axis))]
    return lax.ppermute(value, axis, pairs)


def unit_rows(values):
    return values * lax.rsqrt(jnp.sum(values * values, axis=-1, keepdims=True) + EPS)


def per_device(
    hidden,
    states,
    migration,
    routes,
    w_qkvz,
    w_ba,
    a_log,
    dt_bias,
    attn_gain,
    head_gain,
    w_out,
    moe_gain,
    w_router,
    w_gate_up,
    w_down,
):
    groups = lax.axis_size("dp")
    members = lax.axis_size("expert")
    group = lax.axis_index("dp")
    member = lax.axis_index("expert")
    rows, width = hidden.shape
    depth = w_qkvz.shape[0]
    piece = width // members
    total_rows = routes.shape[0]
    head_state = states[:, 0]

    other_qk = swap_with(w_qkvz[:, :DK], "expert", 1)
    slices = []
    for i in range(groups):
        part = lax.dynamic_slice_in_dim(hidden, (group ^ i) * depth, depth, 1)
        slices.append(part if i == 0 else swap_with(part, "dp", i))
    gain_slice = lax.dynamic_slice_in_dim(attn_gain, group * depth, depth, 0)
    scaled = (jnp.concatenate(slices, axis=0).astype(F32) * gain_slice).astype(BF)

    leave_count = migration.shape[0] // groups
    mine = lax.dynamic_slice_in_dim(migration, group * leave_count, leave_count)
    to_group = mine[None, :, 2] == jnp.arange(groups)[:, None]
    slot_for = jnp.sum(jnp.where(to_group, mine[None, :, 1], 0), axis=1)
    received = lax.all_to_all(
        head_state[slot_for], "dp", split_axis=0, concat_axis=0, tiled=True
    )
    target = jnp.where(migration[:, 2] == group, migration[:, 3], rows)
    head_state = head_state.at[target].set(received[migration[:, 0]], mode="drop")

    partial = jnp.concatenate(
        [
            jnp.dot(scaled, w_qkvz, preferred_element_type=F32),
            jnp.dot(scaled, other_qk, preferred_element_type=F32),
            jnp.pad(jnp.dot(scaled, w_ba, preferred_element_type=F32), ((0, 0), (0, 126))),
        ],
        axis=1,
    )
    summed = partial[:rows]
    for i in range(1, groups):
        summed = summed + swap_with(partial[i * rows : (i + 1) * rows], "dp", i)
    hidden_f32 = hidden.astype(F32)
    scale = lax.rsqrt(jnp.mean(hidden_f32 * hidden_f32, axis=-1, keepdims=True) + EPS)
    projected = (summed * scale).astype(BF).astype(F32)

    own_qk = projected[:, :DK]
    values = projected[:, DK : DK + DV]
    out_gate = projected[:, DK + DV : DK + 2 * DV]
    other = projected[:, DK + 2 * DV : 2 * DK + 2 * DV]
    mix_values = projected[:, 2 * DK + 2 * DV :]
    first = jnp.where(member % 2 == 0, own_qk, other)
    second = jnp.where(member % 2 == 0, other, own_qk)
    half = DK // 2
    queries = unit_rows(jnp.concatenate([first[:, :half], second[:, :half]], axis=1)) * DK ** (-0.5)
    keys_unit = unit_rows(jnp.concatenate([first[:, half:], second[:, half:]], axis=1))
    beta_gate = jax.nn.sigmoid(mix_values[:, 0:1])
    decay_rate = jnp.exp(-jnp.exp(a_log[0]) * jax.nn.softplus(mix_values[:, 1:2] + dt_bias[0]))
    key_sum = jnp.sum(keys_unit[:, :, None] * head_state, axis=1)
    query_sum = jnp.sum(queries[:, :, None] * head_state, axis=1)
    correction = (values - key_sum * decay_rate) * beta_gate
    overlap = jnp.sum(queries * keys_unit, axis=1, keepdims=True)
    readout = query_sum * decay_rate + overlap * correction
    normed = readout * lax.rsqrt(jnp.mean(readout * readout, axis=-1, keepdims=True) + EPS)
    gated = (normed * head_gain * jax.nn.silu(out_gate)).astype(BF)

    attention = jnp.dot(gated, w_out, preferred_element_type=F32).astype(BF)
    attention = jnp.transpose(attention.reshape(rows, members, piece), (1, 0, 2))
    attention = lax.all_to_all(attention, "expert", split_axis=0, concat_axis=0, tiled=True)
    own_hidden = lax.dynamic_slice_in_dim(hidden, member * piece, piece, 1)
    residual = own_hidden.astype(F32) + jnp.sum(attention.astype(F32), axis=0)

    own_gain = lax.dynamic_slice_in_dim(moe_gain, member * piece, piece, 0)
    gained = (residual * own_gain).astype(BF)
    devices = groups * members
    every = lax.all_to_all(
        jnp.broadcast_to(gained[None], (devices, rows, piece)),
        ("dp", "expert"),
        split_axis=0,
        concat_axis=0,
        tiled=True,
    )
    every = every.reshape(groups, members, rows, piece)
    every = jnp.transpose(every, (0, 2, 1, 3)).reshape(total_rows, width)
    ungained = every.astype(F32) / moe_gain
    scale = lax.rsqrt(jnp.mean(ungained * ungained, axis=-1, keepdims=True) + EPS)
    logits = jnp.dot(every, w_router, preferred_element_type=F32) * scale
    gate_up = jnp.dot(every, w_gate_up[0], preferred_element_type=F32) * scale
    hidden_act = (jax.nn.silu(gate_up[:, :MOE_FF]) * gate_up[:, MOE_FF:]).astype(BF)
    output = jnp.dot(hidden_act, w_down[0], preferred_element_type=F32)
    expert_index = group * members + member
    hit = jnp.any(routes == expert_index, axis=1, keepdims=True)
    weight = jnp.where(hit, jnp.exp(logits), 0.0)
    weighted = (weight * output).astype(BF)

    weighted = jnp.transpose(weighted.reshape(groups, rows, members, piece), (0, 2, 1, 3))
    weighted = weighted.reshape(devices, rows * piece)
    high = weight.astype(BF)
    low = (weight - high.astype(F32)).astype(BF)
    tail = jnp.concatenate([high.reshape(groups, 1, rows), low.reshape(groups, 1, rows)], axis=2)
    tail = jnp.broadcast_to(tail, (groups, members, 2 * rows)).reshape(devices, 2 * rows)
    tail = jnp.pad(tail, ((0, 0), (0, 1024 - 2 * rows)))
    sent = jnp.concatenate([weighted, tail], axis=1).reshape(devices, -1, 128)
    back = lax.all_to_all(sent, ("dp", "expert"), split_axis=0, concat_axis=0, tiled=True)
    back = jnp.sum(back.reshape(devices, -1).astype(F32), axis=0)
    numerator = back[: rows * piece].reshape(rows, piece)
    denominator = back[rows * piece : rows * piece + rows] + back[rows * piece + rows : rows * piece + 2 * rows]
    return (residual + numerator / denominator[:, None]).astype(BF)


def solution(mesh):
    placed = (
        P(("parts", "dp"), None),
        P(("parts", "dp"), "expert", None, None),
        P("parts", None),
        P("parts", None),
        P("dp", "expert"),
        P("dp", "expert"),
        P("expert"),
        P("expert"),
        P(),
        P(),
        P("expert", None),
        P(),
        P(None, ("dp", "expert")),
        P(("dp", "expert"), None, None),
        P(("dp", "expert"), None, None),
    )
    return jax.shard_map(
        per_device,
        mesh=mesh,
        in_specs=placed,
        out_specs=P(("parts", "dp"), "expert"),
        check_vma=False,
    )
```

```python
import functools

import jax
import jax.numpy as jnp
from jax import lax
from jax.experimental import pallas as pl
from jax.experimental.pallas import tpu as pltpu
from jax.sharding import PartitionSpec as P

DK = 128
DV = 128
MOE_FF = 256
LANES = 128
SENT = 2 * DK + 2 * DV + LANES

EPS = 1e-06
BF = jnp.bfloat16
F32 = jnp.float32

VMEM = pl.BlockSpec(memory_space=pltpu.VMEM)
SMEM = pl.BlockSpec(memory_space=pltpu.SMEM)
HBM = pl.BlockSpec(memory_space=pltpu.HBM)
ANY = pl.BlockSpec(memory_space=pl.ANY)
COST = pl.CostEstimate(flops=0, bytes_accessed=8 * 1024 * 1024, transcendentals=0)
PARAMS = pltpu.CompilerParams(vmem_limit_bytes=24 * 1024 * 1024)


def in_hbm(*values):
    return [pltpu.with_memory_space_constraint(value, pltpu.HBM) for value in values]


def copy_all(pairs, sems):
    copies = [pltpu.make_async_copy(a, b, sems.at[i]) for i, (a, b) in enumerate(pairs)]
    for copy in copies:
        copy.start()
    return copies


def swap_with(value, axis, offset):
    pairs = [(source, source ^ offset) for source in range(lax.axis_size(axis))]
    return lax.ppermute(value, axis, pairs)


def row_scale(values):
    return lax.rsqrt(jnp.mean(values * values, axis=-1, keepdims=True) + EPS)


def unit_rows(values):
    return values * lax.rsqrt(jnp.sum(values * values, axis=-1, keepdims=True) + EPS)


def group_index():
    return lax.axis_index("x") * lax.axis_size("core") + lax.axis_index("core")


def pieces_kernel(groups, hidden, w_qkvz, *refs):
    own_qk, pieces, sems = refs[0], refs[1:-1], refs[-1]
    group = group_index()
    depth = w_qkvz.shape[0]
    pairs = [(w_qkvz.at[:, pl.ds(0, DK)], own_qk)]
    for i in range(1, groups):
        first = pl.multiple_of((group ^ i) * depth, depth)
        pairs.append((hidden.at[:, pl.ds(first, depth)], pieces[i - 1]))
    for copy in copy_all(pairs, sems):
        copy.wait()


def leaving_kernel(groups, leave_count, migration, states, early, *refs):
    count = (len(refs) - groups - 3) // 2
    sources, leaving, staged = refs[:count], refs[count : count + groups], refs[count + groups : -3]
    plan, plan_sem, sems = refs[-3:]
    del early
    plan_copy = pltpu.make_async_copy(migration, plan, plan_sem)
    plan_copy.start()
    copies = copy_all(list(zip(sources, staged)), sems)
    group = group_index()
    plan_copy.wait()
    for i in range(groups):
        slot = 0
        for j in range(leave_count):
            at = group * leave_count + j
            slot = jnp.where(plan[2, at] == (group ^ i), plan[1, at], slot)
        copy = pltpu.make_async_copy(states.at[slot, 0], leaving[i], sems.at[count + i])
        copy.start()
        copies.append(copy)
    for copy in copies:
        copy.wait()


def project_kernel(groups, hidden, gain, w_ba, w_qkvz, other_qk, *refs):
    pieces, outs, scaled = refs[: groups - 1], refs[groups - 1 : -1], refs[-1]
    group = group_index()
    depth = w_qkvz.shape[0]
    rows = hidden.shape[0]
    columns = pl.ds(pl.multiple_of(group * depth, depth), depth)
    own_gain = gain[:, columns]
    for i in range(groups):
        part = hidden[:, columns] if i == 0 else pieces[i - 1][...]
        scaled[i * rows : (i + 1) * rows, :] = (part.astype(F32) * own_gain).astype(BF)
    x = scaled[...]
    main = jnp.dot(x, w_qkvz[...], preferred_element_type=F32)
    other = jnp.dot(x, other_qk[...], preferred_element_type=F32)
    wide = x.astype(F32)
    lane = lax.broadcasted_iota(jnp.int32, (groups * rows, LANES), 1)
    mixes = jnp.zeros((groups * rows, LANES), F32)
    for j in range(2):
        total = jnp.sum(wide * w_ba[j : j + 1, :].astype(F32), axis=1, keepdims=True)
        mixes = jnp.where(lane == j, total, mixes)
    for i in range(groups):
        block = slice(i * rows, (i + 1) * rows)
        outs[i][:, : DK + 2 * DV] = main[block]
        outs[i][:, DK + 2 * DV : 2 * DK + 2 * DV] = other[block]
        outs[i][:, 2 * DK + 2 * DV :] = mixes[block]


def settle_kernel(groups, leave_count, migration, states, hidden, gain, routes, after, *refs):
    arrivals, refs = refs[:groups], refs[groups:]
    held, scale, own_hidden, own_gain, hits = refs[-8:-3]
    rest = refs[:-8]
    count = len(rest) // 2
    plan, plan_sem, sems = refs[-3:]
    del after
    plan_copy = pltpu.make_async_copy(migration, plan, plan_sem)
    plan_copy.start()
    copies = copy_all([(states.at[:, 0], held)] + list(zip(rest[:count], rest[count:])), sems)
    group = group_index()
    core = lax.axis_index("core")
    member = lax.axis_index("expert")
    rows = hidden.shape[0]
    total_rows = groups * rows
    piece = own_hidden.shape[1]
    members = hidden.shape[1] // piece
    wide = hidden[...].astype(F32)
    scale[...] = jnp.broadcast_to(row_scale(wide), scale.shape)
    own, own_g = wide[:, :piece], gain[:, :piece]
    for m in range(1, members):
        columns = slice(m * piece, (m + 1) * piece)
        own = jnp.where(member == m, wide[:, columns], own)
        own_g = jnp.where(member == m, gain[:, columns], own_g)
    own_hidden[...] = own
    own_gain[...] = own_g
    found = jnp.where(routes[...] == group * members + member, 1.0, 0.0)
    found = jnp.max(found, axis=0, keepdims=True)
    row = lax.broadcasted_iota(jnp.int32, (total_rows, total_rows), 0)
    lane = lax.broadcasted_iota(jnp.int32, (total_rows, total_rows), 1)
    block, slot = row // rows, row % rows
    source_group = 2 * (block % (groups // 2)) + (core ^ (block // (groups // 2)))
    same = lane == source_group * rows + slot
    column = jnp.sum(jnp.where(same, found, 0.0), axis=1, keepdims=True)
    hits[...] = jnp.broadcast_to(column, hits.shape)
    plan_copy.wait()
    for copy in copies:
        copy.wait()
    for i in range(groups):
        for j in range(leave_count):
            at = (group ^ i) * leave_count + j

            @pl.when(plan[2, at] == group)
            def _():
                held[plan[3, at]] = arrivals[i][...]


def delta_kernel(a_log, dt_bias, scale, head_gain, w_out, held, *refs):
    partials, (out, key_sums, query_sums) = refs[:-3], refs[-3:]
    member = lax.axis_index("expert")
    rows = held.shape[0]
    summed = partials[0][...]
    for partial in partials[1:]:
        summed = summed + partial[...]
    projected = (summed * scale[:, 0:1]).astype(BF).astype(F32)
    own_qk = projected[:, :DK]
    values = projected[:, DK : DK + DV]
    out_gate = projected[:, DK + DV : DK + 2 * DV]
    other = projected[:, DK + 2 * DV : 2 * DK + 2 * DV]
    write_mix = projected[:, 2 * DK + 2 * DV : 2 * DK + 2 * DV + 1]
    decay_mix = projected[:, 2 * DK + 2 * DV + 1 : 2 * DK + 2 * DV + 2]
    is_first = member % 2 == 0
    first = jnp.where(is_first, own_qk, other)
    second = jnp.where(is_first, other, own_qk)
    low_half = lax.broadcasted_iota(jnp.int32, (rows, DK), 1) < DK // 2
    queries = unit_rows(jnp.where(low_half, first, pltpu.roll(second, DK // 2, 1))) * DK ** (-0.5)
    keys_unit = unit_rows(jnp.where(low_half, pltpu.roll(first, DK // 2, 1), second))
    shifted = decay_mix + dt_bias[0]
    soft = jnp.maximum(shifted, 0.0) + jnp.log1p(jnp.exp(-jnp.abs(shifted)))
    decay = jnp.exp(-jnp.exp(jnp.full((rows, 1), a_log[0], F32)) * soft)
    beta = jax.nn.sigmoid(write_mix)
    keys_t = jnp.transpose(keys_unit)
    queries_t = jnp.transpose(queries)
    for r in range(rows):
        state = held[r]
        key_sums[r : r + 1, :] = jnp.sum(state * keys_t[:, r : r + 1], axis=0, keepdims=True)
        query_sums[r : r + 1, :] = jnp.sum(state * queries_t[:, r : r + 1], axis=0, keepdims=True)
    correction = (values - key_sums[...] * decay) * beta
    overlap = jnp.sum(queries * keys_unit, axis=1, keepdims=True)
    readout = query_sums[...] * decay + overlap * correction
    normed = readout * row_scale(readout) * head_gain[...]
    gated = (normed * (out_gate * jax.nn.sigmoid(out_gate))).astype(BF)
    attention = jnp.dot(gated, w_out[...], preferred_element_type=F32).astype(BF)
    piece = out.shape[2]
    for m in range(out.shape[0]):
        out[m] = attention[:, m * piece : (m + 1) * piece]


def residual_kernel(attention, hidden, gain, gained, residual):
    members, rows, piece = attention.shape
    total = hidden[...]
    for m in range(members):
        total = total + attention[m].astype(F32)
    residual[...] = total
    sent = (total * gain[...]).astype(BF)
    for d in range(gained.shape[0]):
        gained[d] = sent


def packed(tile, piece):
    if piece >= LANES:
        return [tile[:, c : c + LANES] for c in range(0, piece, LANES)]
    count = LANES // piece
    part = tile.shape[0] // count
    return [jnp.concatenate([tile[c * part : (c + 1) * part] for c in range(count)], axis=1)]


def unpacked(tile, rows, piece):
    if piece >= LANES:
        return jnp.concatenate(
            [tile[c * rows : (c + 1) * rows] for c in range(piece // LANES)], axis=1
        )
    return jnp.concatenate([tile[:, c : c + piece] for c in range(0, LANES, piece)], axis=0)


def tail_of(weight):
    part = 8
    lane = lax.broadcasted_iota(jnp.int32, (part, LANES), 1)
    tail = jnp.zeros((part, LANES), F32)
    for c in range(weight.shape[0] // part):
        at = weight[c * part : (c + 1) * part]
        high = at.astype(BF).astype(F32)
        tail = jnp.where(lane == c, high, tail)
        tail = jnp.where(lane == LANES // 2 + c, at - high, tail)
    return tail


def expert_kernel(width, every, across, hits, gain, w_router, w_gate_up, w_down, out, out_across):
    devices, rows, piece = every.shape
    members = width // piece
    half = devices // members
    total_rows = 2 * half * rows
    gate_up = jnp.zeros((total_rows, 2 * MOE_FF), F32)
    squares = jnp.zeros((total_rows, piece), F32)
    routed = jnp.zeros((total_rows, piece), F32)
    inverse = 1.0 / gain[...]
    for m in range(members):
        columns = slice(m * piece, (m + 1) * piece)
        x = jnp.concatenate(
            [ref[g * members + m] for ref in (every, across) for g in range(half)], axis=0
        )
        gate_up = gate_up + jnp.dot(x, w_gate_up[0, columns, :], preferred_element_type=F32)
        wide = x.astype(F32)
        plain = wide * inverse[:, columns]
        squares = squares + plain * plain
        routed = routed + wide * w_router[:, columns].astype(F32)
    scale = lax.rsqrt(jnp.sum(squares, axis=1, keepdims=True) * (1.0 / width) + EPS)
    logits = jnp.sum(routed, axis=1, keepdims=True) * scale
    weight = jnp.where(hits[:, 0:1] > 0.0, jnp.exp(logits), 0.0)
    gate_up = gate_up * scale
    gate = gate_up[:, :MOE_FF]
    act = (gate * jax.nn.sigmoid(gate) * gate_up[:, MOE_FF:]).astype(BF)
    tails = [tail_of(weight[g * rows : (g + 1) * rows]) for g in range(2 * half)]
    step = max(piece, LANES)
    for start in range(0, width, step):
        y = jnp.dot(act, w_down[0, :, start : start + step], preferred_element_type=F32) * weight
        for m in range(step // piece):
            for g in range(2 * half):
                tile = y[g * rows : (g + 1) * rows, m * piece : (m + 1) * piece]
                target = out if g < half else out_across
                target[g % half * members + start // piece + m] = jnp.concatenate(
                    packed(tile, piece) + [tails[g]], axis=0
                ).astype(BF)


def pair_kernel(own, received, out):
    devices, height, _ = own.shape
    body = height - 8
    low_half = lax.broadcasted_iota(jnp.int32, (8, LANES), 1) < LANES // 2
    for d in range(devices):
        total = own[d].astype(F32) + received[d].astype(F32)
        tail = total[body:]
        tail = tail + pltpu.roll(tail, LANES // 2, 1)
        high = tail.astype(BF).astype(F32)
        tail = jnp.where(low_half, high, tail - high)
        out[d] = jnp.concatenate([total[:body], tail], axis=0).astype(BF)


def final_kernel(back, residual, out):
    devices, height, _ = back.shape
    rows, piece = residual.shape
    total = back[0].astype(F32)
    for d in range(1, devices):
        total = total + back[d].astype(F32)
    body = rows * piece // LANES
    numerator = unpacked(total[:body], rows, piece)
    tail = total[body:]
    tail = tail + pltpu.roll(tail, LANES // 2, 1)
    denominator = jnp.concatenate(
        [tail[:, c : c + 1] for c in range(rows // tail.shape[0])], axis=0
    )
    out[...] = (residual[...] + numerator / denominator).astype(BF)


def per_device(
    hidden,
    states,
    migration,
    routes,
    w_qkvz,
    w_ba,
    a_log,
    dt_bias,
    attn_gain,
    head_gain,
    w_out,
    moe_gain,
    w_router,
    w_gate_up,
    w_down,
):
    dp = ("x", "core")
    half = lax.axis_size("x")
    groups = half * lax.axis_size("core")
    members = lax.axis_size("expert")
    rows, width = hidden.shape
    depth = w_qkvz.shape[0]
    piece = width // members
    total_rows = routes.shape[0]
    leave_count = migration.shape[0] // groups
    plan = jnp.transpose(migration)
    shape = jax.ShapeDtypeStruct

    own_qk, *pieces = pl.pallas_call(
        functools.partial(pieces_kernel, groups),
        out_shape=[pltpu.VMEM((depth, DK), BF)] + [pltpu.VMEM((rows, depth), BF)] * (groups - 1),
        in_specs=[HBM] * 2,
        out_specs=[VMEM] * groups,
        scratch_shapes=[pltpu.SemaphoreType.DMA((groups,))],
        compiler_params=PARAMS,
        cost_estimate=COST,
        name="pieces",
    )(*in_hbm(hidden, w_qkvz))
    other_qk = swap_with(own_qk, "expert", 1)
    pieces = [swap_with(piece_i, dp, i + 1) for i, piece_i in enumerate(pieces)]
    operands = [hidden, w_qkvz, attn_gain.reshape(1, width), jnp.transpose(w_ba)]
    left = pl.pallas_call(
        functools.partial(leaving_kernel, groups, leave_count),
        out_shape=[pltpu.VMEM((DK, DV), F32)] * groups
        + [pltpu.VMEM(operand.shape, operand.dtype) for operand in operands],
        in_specs=[HBM, HBM, ANY] + [HBM] * len(operands),
        out_specs=[VMEM] * (groups + len(operands)),
        scratch_shapes=[
            pltpu.SMEM(plan.shape, jnp.int32),
            pltpu.SemaphoreType.DMA,
            pltpu.SemaphoreType.DMA((groups + len(operands),)),
        ],
        compiler_params=PARAMS,
        cost_estimate=COST,
        name="leaving",
    )(*in_hbm(plan, states), pieces[0], *in_hbm(*operands))
    leaving, (hidden_near, w_near, attn_gain_near, w_ba_near) = left[:groups], left[groups:]
    arrivals = [leaving[0]] + [swap_with(leaving[i], dp, i) for i in range(1, groups)]

    partials = pl.pallas_call(
        functools.partial(project_kernel, groups),
        out_shape=[pltpu.VMEM((rows, SENT), F32)] * groups,
        in_specs=[VMEM] * (groups + 4),
        out_specs=[VMEM] * groups,
        scratch_shapes=[pltpu.VMEM((total_rows, depth), BF)],
        compiler_params=PARAMS,
        cost_estimate=COST,
        name="project",
    )(hidden_near, attn_gain_near, w_ba_near, w_near, other_qk, *pieces)
    after = partials[0]
    partials = [partials[0]] + [swap_with(partials[i], dp, i) for i in range(1, groups)]
    operands = [
        w_out,
        head_gain.reshape(1, DV),
        moe_gain.reshape(1, width),
        jnp.transpose(w_router),
    ]
    settled = pl.pallas_call(
        functools.partial(settle_kernel, groups, leave_count),
        out_shape=[pltpu.VMEM(operand.shape, operand.dtype) for operand in operands]
        + [
            pltpu.VMEM((rows, DK, DV), F32),
            pltpu.VMEM((rows, LANES), F32),
            pltpu.VMEM((rows, piece), F32),
            pltpu.VMEM((1, piece), F32),
            pltpu.VMEM((total_rows, LANES), F32),
        ],
        in_specs=[HBM, HBM, VMEM, VMEM, VMEM, ANY] + [VMEM] * groups + [HBM] * len(operands),
        out_specs=[VMEM] * (5 + len(operands)),
        scratch_shapes=[
            pltpu.SMEM(plan.shape, jnp.int32),
            pltpu.SemaphoreType.DMA,
            pltpu.SemaphoreType.DMA((1 + len(operands),)),
        ],
        compiler_params=PARAMS,
        cost_estimate=COST,
        name="settle",
    )(
        *in_hbm(plan, states),
        hidden_near,
        *in_hbm(moe_gain.reshape(1, width), jnp.transpose(routes)),
        after,
        *arrivals,
        *in_hbm(*operands),
    )
    w_out_near, head_gain_near, moe_gain_near, router_near = settled[:-5]
    held, scale, own_hidden, own_gain, hits = settled[-5:]

    attention = pl.pallas_call(
        delta_kernel,
        out_shape=pltpu.VMEM((members, rows, piece), BF),
        in_specs=[SMEM] * 2 + [VMEM] * (4 + groups),
        out_specs=VMEM,
        scratch_shapes=[pltpu.VMEM((rows, DV), F32)] * 2,
        compiler_params=PARAMS,
        cost_estimate=COST,
        name="delta",
    )(a_log, dt_bias, scale, head_gain_near, w_out_near, held, *partials)
    attention = lax.all_to_all(attention, "expert", split_axis=0, concat_axis=0, tiled=True)

    gained, residual = pl.pallas_call(
        residual_kernel,
        out_shape=[
            pltpu.VMEM((half * members, rows, piece), BF),
            pltpu.VMEM((rows, piece), F32),
        ],
        in_specs=[VMEM] * 3,
        out_specs=[VMEM] * 2,
        compiler_params=PARAMS,
        cost_estimate=COST,
        name="residual",
    )(attention, own_hidden, own_gain)
    every = lax.all_to_all(gained, ("x", "expert"), split_axis=0, concat_axis=0, tiled=True)
    across = swap_with(every, "core", 1)

    height = rows * piece // LANES + 8
    sent, sent_across = pl.pallas_call(
        functools.partial(expert_kernel, width),
        out_shape=[pltpu.VMEM((half * members, height, LANES), BF)] * 2,
        in_specs=[VMEM] * 7,
        out_specs=[VMEM] * 2,
        compiler_params=PARAMS,
        cost_estimate=COST,
        name="experts",
    )(
        every,
        across,
        hits,
        moe_gain_near,
        router_near,
        w_gate_up,
        w_down,
    )
    sent = pl.pallas_call(
        pair_kernel,
        out_shape=pltpu.VMEM((half * members, height, LANES), BF),
        in_specs=[VMEM] * 2,
        out_specs=VMEM,
        compiler_params=PARAMS,
        cost_estimate=COST,
        name="pair",
    )(sent, swap_with(sent_across, "core", 1))
    back = lax.all_to_all(sent, ("x", "expert"), split_axis=0, concat_axis=0, tiled=True)
    return pl.pallas_call(
        final_kernel,
        out_shape=shape((rows, piece), BF),
        in_specs=[VMEM] * 2,
        out_specs=VMEM,
        compiler_params=PARAMS,
        cost_estimate=COST,
        name="finish",
    )(back, residual)


def solution(mesh):
    parts, groups, members = (mesh.shape[name] for name in ("parts", "dp", "expert"))
    devices = mesh.devices.reshape(parts, groups // 2, 2, members)
    fine = jax.sharding.Mesh(devices, ("parts", "x", "core", "expert"))
    placed = (
        P(("parts", "x", "core"), None),
        P(("parts", "x", "core"), "expert", None, None),
        P("parts", None),
        P("parts", None),
        P(("x", "core"), "expert"),
        P(("x", "core"), "expert"),
        P("expert"),
        P("expert"),
        P(),
        P(),
        P("expert", None),
        P(),
        P(None, ("x", "core", "expert")),
        P(("x", "core", "expert"), None, None),
        P(("x", "core", "expert"), None, None),
    )
    return jax.shard_map(
        per_device,
        mesh=fine,
        in_specs=placed,
        out_specs=P(("parts", "x", "core"), "expert"),
        check_vma=False,
    )
```

```python
import functools

import jax
import jax.numpy as jnp
from jax import lax
from jax.experimental import pallas as pl
from jax.experimental.pallas import tpu as pltpu
from jax.sharding import PartitionSpec as P

DK = 128
DV = 128
MOE_FF = 256
LANES = 128
SENT = 2 * DK + 2 * DV + LANES

EPS = 1e-06
BF = jnp.bfloat16
F32 = jnp.float32

VMEM = pl.BlockSpec(memory_space=pltpu.VMEM)
SMEM = pl.BlockSpec(memory_space=pltpu.SMEM)
HBM = pl.BlockSpec(memory_space=pltpu.HBM)
ANY = pl.BlockSpec(memory_space=pl.ANY)
COST = pl.CostEstimate(flops=0, bytes_accessed=8 * 1024 * 1024, transcendentals=0)
PARAMS = pltpu.CompilerParams(vmem_limit_bytes=24 * 1024 * 1024)


def in_hbm(*values):
    return [pltpu.with_memory_space_constraint(value, pltpu.HBM) for value in values]


def copy_all(pairs, sems):
    copies = [pltpu.make_async_copy(a, b, sems.at[i]) for i, (a, b) in enumerate(pairs)]
    for copy in copies:
        copy.start()
    return copies


def swap_with(value, axis, offset):
    pairs = [(source, source ^ offset) for source in range(lax.axis_size(axis))]
    return lax.ppermute(value, axis, pairs)


def row_scale(values):
    return lax.rsqrt(jnp.mean(values * values, axis=-1, keepdims=True) + EPS)


def unit_rows(values):
    return values * lax.rsqrt(jnp.sum(values * values, axis=-1, keepdims=True) + EPS)


def group_index():
    return lax.axis_index("x") * lax.axis_size("core") + lax.axis_index("core")


def first_kernel(groups, leave_count, migration, states, hidden, w_qkvz, *refs):
    gain, w_ba, own_qk, messages = refs[0], refs[1], refs[2], refs[3 : groups + 2]
    held, hidden_near, w_near, w_ba_near, normed, gain_near, plan, plan_sem, sems = refs[groups + 2 :]
    plan_copy = pltpu.make_async_copy(migration, plan, plan_sem)
    plan_copy.start()
    pairs = [
        (hidden, hidden_near),
        (states.at[:, 0], held),
        (w_qkvz.at[:, pl.ds(0, DK)], own_qk),
        (w_qkvz, w_near),
        (gain, gain_near),
        (w_ba, w_ba_near),
    ]
    copies = copy_all(pairs, sems)
    group = group_index()
    rows = hidden.shape[0]
    depth = w_qkvz.shape[0]
    tiles = depth // LANES
    copies[0].wait()
    wide = hidden_near[...].astype(F32)
    copies[4].wait()
    normed[...] = (wide * row_scale(wide) * gain_near[...]).astype(BF)
    for i in range(1, groups):
        for c in range(tiles):
            first = pl.multiple_of((group ^ i) * depth + c * LANES, LANES)
            messages[i - 1][c * rows : (c + 1) * rows, :] = normed[:, pl.ds(first, LANES)]
    plan_copy.wait()
    copies[1].wait()
    for i in range(1, groups):
        slot = 0
        for j in range(leave_count):
            at = group * leave_count + j
            slot = jnp.where(plan[2, at] == (group ^ i), plan[1, at], slot)
        messages[i - 1][tiles * rows :, :] = held[slot].astype(BF)
    for copy in copies[2:4] + copies[5:]:
        copy.wait()


def project_kernel(groups, normed, w_ba, w_qkvz, other_qk, staged, *refs):
    messages, outs, scaled = refs[: groups - 1], refs[groups - 1 : -1], refs[-1]
    del staged
    group = group_index()
    depth = w_qkvz.shape[0]
    rows = normed.shape[0]
    for c in range(depth // LANES):
        columns = pl.ds(pl.multiple_of(group * depth + c * LANES, LANES), LANES)
        for i in range(groups):
            part = normed[:, columns] if i == 0 else messages[i - 1][c * rows : (c + 1) * rows, :]
            scaled[i * rows : (i + 1) * rows, c * LANES : (c + 1) * LANES] = part
    x = scaled[...]
    main = jnp.dot(x, w_qkvz[...], preferred_element_type=F32)
    other = jnp.dot(x, other_qk[...], preferred_element_type=F32)
    wide = x.astype(F32)
    lane = lax.broadcasted_iota(jnp.int32, (groups * rows, LANES), 1)
    mixes = jnp.zeros((groups * rows, LANES), F32)
    for j in range(2):
        total = jnp.sum(wide * w_ba[j : j + 1, :].astype(F32), axis=1, keepdims=True)
        mixes = jnp.where(lane == j, total, mixes)
    for i in range(groups):
        block = slice(i * rows, (i + 1) * rows)
        outs[i][:, : DK + 2 * DV] = main[block]
        outs[i][:, DK + 2 * DV : 2 * DK + 2 * DV] = other[block]
        outs[i][:, 2 * DK + 2 * DV :] = mixes[block]


def stage_kernel(groups, hidden, gain, routes, router, w_gate_up, w_down, *refs):
    count = (len(refs) - 5) // 2
    sources, staged = refs[:count], refs[count : 2 * count]
    own_hidden, own_gain, hits, expert, sems = refs[-5:]
    width = hidden.shape[1]
    span = 2 * MOE_FF
    pairs = [(w_gate_up.at[0], expert.at[pl.ds(0, width)])]
    for c in range(width // span):
        pairs.append(
            (
                w_down.at[0, :, pl.ds(c * span, span)],
                expert.at[pl.ds(width + c * MOE_FF, MOE_FF)],
            )
        )
    copies = copy_all(list(zip(sources, staged)) + pairs, sems)
    line = lax.broadcasted_iota(jnp.int32, (16, span), 0)
    block = jnp.zeros((16, span), F32)
    for c in range(width // span):
        block = jnp.where(line == c, router[:, c * span : (c + 1) * span].astype(F32), block)
    expert[expert.shape[0] - 16 :, :] = block.astype(BF)
    group = group_index()
    core = lax.axis_index("core")
    member = lax.axis_index("expert")
    rows = hidden.shape[0]
    total_rows = groups * rows
    piece = own_hidden.shape[1]
    members = width // piece
    own, own_g = hidden[:, :piece], gain[:, :piece]
    for m in range(1, members):
        columns = slice(m * piece, (m + 1) * piece)
        own = jnp.where(member == m, hidden[:, columns], own)
        own_g = jnp.where(member == m, gain[:, columns], own_g)
    own_hidden[...] = own.astype(F32)
    own_gain[...] = own_g
    served = total_rows // 2
    row = lax.broadcasted_iota(jnp.int32, (served, total_rows), 0)
    lane = lax.broadcasted_iota(jnp.int32, (served, total_rows), 1)
    same = lane == (2 * (row // rows) + core) * rows + row % rows
    at = lax.broadcasted_iota(jnp.int32, hits.shape, 1)
    table = jnp.zeros(hits.shape, F32)
    for i in range(2):
        found = jnp.where(routes[...] == (group ^ i) * members + member, 1.0, 0.0)
        found = jnp.max(found, axis=0, keepdims=True)
        column = jnp.sum(jnp.where(same, found, 0.0), axis=1, keepdims=True)
        table = jnp.where(at == i, column, table)
    hits[...] = table
    for copy in copies:
        copy.wait()


def settle_kernel(groups, leave_count, migration, a_log, dt_bias, states, after, *refs):
    messages, (held, mixing, own_state, plan, plan_sem) = refs[:-5], refs[-5:]
    del after
    plan_copy = pltpu.make_async_copy(migration, plan, plan_sem)
    plan_copy.start()
    mixing[0:1, :] = jnp.exp(jnp.full((1, LANES), a_log[0], F32))
    mixing[1:2, :] = jnp.full((1, LANES), dt_bias[0], F32)
    group = group_index()
    plan_copy.wait()
    for j in range(leave_count):
        at = group * leave_count + j

        @pl.when(plan[2, at] == group)
        def _():
            own_state[...] = states[plan[1, at]]

    for i in range(groups):
        for j in range(leave_count):
            at = (group ^ i) * leave_count + j

            @pl.when(plan[2, at] == group)
            def _():
                if i == 0:
                    held[plan[3, at]] = own_state[...]
                else:
                    arrival = messages[i - 1]
                    held[plan[3, at]] = arrival[arrival.shape[0] - DK :, :].astype(F32)


def delta_kernel(mixing, head_gain, w_out, held, expert, *refs):
    partials, (out, passed, key_sums, query_sums) = refs[:-4], refs[-4:]
    del expert, passed
    member = lax.axis_index("expert")
    rows = held.shape[0]
    summed = partials[0][...]
    for partial in partials[1:]:
        summed = summed + partial[...]
    projected = summed.astype(BF).astype(F32)
    own_qk = projected[:, :DK]
    values = projected[:, DK : DK + DV]
    out_gate = projected[:, DK + DV : DK + 2 * DV]
    other = projected[:, DK + 2 * DV : 2 * DK + 2 * DV]
    write_mix = projected[:, 2 * DK + 2 * DV : 2 * DK + 2 * DV + 1]
    decay_mix = projected[:, 2 * DK + 2 * DV + 1 : 2 * DK + 2 * DV + 2]
    is_first = member % 2 == 0
    first = jnp.where(is_first, own_qk, other)
    second = jnp.where(is_first, other, own_qk)
    low_half = lax.broadcasted_iota(jnp.int32, (rows, DK), 1) < DK // 2
    queries = unit_rows(jnp.where(low_half, first, pltpu.roll(second, DK // 2, 1))) * DK ** (-0.5)
    keys_unit = unit_rows(jnp.where(low_half, pltpu.roll(first, DK // 2, 1), second))
    shifted = decay_mix + mixing[1:2, 0:1]
    soft = jnp.maximum(shifted, 0.0) + jnp.log1p(jnp.exp(-jnp.abs(shifted)))
    decay = jnp.exp(-mixing[0:1, 0:1] * soft)
    beta = jax.nn.sigmoid(write_mix)
    keys_t = jnp.transpose(keys_unit)
    queries_t = jnp.transpose(queries)
    for r in range(rows):
        state = held[r]
        key_sums[r : r + 1, :] = jnp.sum(state * keys_t[:, r : r + 1], axis=0, keepdims=True)
        query_sums[r : r + 1, :] = jnp.sum(state * queries_t[:, r : r + 1], axis=0, keepdims=True)
    correction = (values - key_sums[...] * decay) * beta
    overlap = jnp.sum(queries * keys_unit, axis=1, keepdims=True)
    readout = query_sums[...] * decay + overlap * correction
    normed = readout * row_scale(readout) * head_gain[...]
    gated = (normed * (out_gate * jax.nn.sigmoid(out_gate))).astype(BF)
    attention = jnp.dot(gated, w_out[...], preferred_element_type=F32).astype(BF)
    piece = out.shape[2]
    for m in range(out.shape[0]):
        out[m] = attention[:, m * piece : (m + 1) * piece]


def residual_kernel(attention, hidden, gain, gained, residual):
    members, rows, piece = attention.shape
    total = hidden[...]
    for m in range(members):
        total = total + attention[m].astype(F32)
    residual[...] = total
    sent = (total * gain[...]).astype(BF)
    for d in range(gained.shape[0]):
        gained[d] = sent


def packed(tile, piece):
    if piece >= LANES:
        return [tile[:, c : c + LANES] for c in range(0, piece, LANES)]
    count = LANES // piece
    part = tile.shape[0] // count
    return [jnp.concatenate([tile[c * part : (c + 1) * part] for c in range(count)], axis=1)]


def unpacked(tile, rows, piece):
    if piece >= LANES:
        return jnp.concatenate(
            [tile[c * rows : (c + 1) * rows] for c in range(piece // LANES)], axis=1
        )
    return jnp.concatenate([tile[:, c : c + piece] for c in range(0, LANES, piece)], axis=0)


def tail_of(weight):
    part = 8
    lane = lax.broadcasted_iota(jnp.int32, (part, LANES), 1)
    tail = jnp.zeros((part, LANES), F32)
    for c in range(weight.shape[0] // part):
        at = weight[c * part : (c + 1) * part]
        high = at.astype(BF).astype(F32)
        tail = jnp.where(lane == c, high, tail)
        tail = jnp.where(lane == LANES // 2 + c, at - high, tail)
    return tail


def expert_kernel(width, every, hits, gain, own, other, out):
    devices, rows, piece = every.shape
    members = width // piece
    half = devices // members
    total_rows = half * rows
    span = 2 * MOE_FF
    experts = (own, other)
    gate_up = [jnp.zeros((total_rows, span), F32)] * 2
    routed = [jnp.zeros((total_rows, piece), F32)] * 2
    squares = jnp.zeros((total_rows, piece), F32)
    inverse = 1.0 / gain[...]
    last = own.shape[0] - 16
    routers = [ref[last:, :].astype(F32) for ref in experts]
    for m in range(members):
        columns = slice(m * piece, (m + 1) * piece)
        line, first = m * piece // span, m * piece % span
        x = jnp.concatenate([every[g * members + m] for g in range(half)], axis=0)
        wide = x.astype(F32)
        plain = wide * inverse[:, columns]
        squares = squares + plain * plain
        for i in range(2):
            gate_up[i] = gate_up[i] + jnp.dot(x, experts[i][columns, :], preferred_element_type=F32)
            routed[i] = routed[i] + wide * routers[i][line : line + 1, first : first + piece]
    scale = lax.rsqrt(jnp.sum(squares, axis=1, keepdims=True) * (1.0 / width) + EPS)
    weights, acts = [], []
    for i in range(2):
        logits = jnp.sum(routed[i], axis=1, keepdims=True) * scale
        weights.append(jnp.where(hits[:, i : i + 1] > 0.0, jnp.exp(logits), 0.0))
        both = gate_up[i] * scale
        gate = both[:, :MOE_FF]
        acts.append((gate * jax.nn.sigmoid(gate) * both[:, MOE_FF:]).astype(BF))
    summed = weights[0] + weights[1]
    tails = [tail_of(summed[g * rows : (g + 1) * rows]) for g in range(half)]
    for c in range(width // span):
        down = slice(width + c * MOE_FF, width + (c + 1) * MOE_FF)
        y = jnp.zeros((total_rows, span), F32)
        for i in range(2):
            y = y + jnp.dot(acts[i], experts[i][down, :], preferred_element_type=F32) * weights[i]
        for m in range(span // piece):
            for g in range(half):
                tile = y[g * rows : (g + 1) * rows, m * piece : (m + 1) * piece]
                out[g * members + c * span // piece + m] = jnp.concatenate(
                    packed(tile, piece) + [tails[g]], axis=0
                ).astype(BF)


def final_kernel(back, residual, out):
    devices, height, _ = back.shape
    rows, piece = residual.shape
    total = back[0].astype(F32)
    for d in range(1, devices):
        total = total + back[d].astype(F32)
    body = rows * piece // LANES
    numerator = unpacked(total[:body], rows, piece)
    tail = total[body:]
    tail = tail + pltpu.roll(tail, LANES // 2, 1)
    denominator = jnp.concatenate(
        [tail[:, c : c + 1] for c in range(rows // tail.shape[0])], axis=0
    )
    out[...] = (residual[...] + numerator / denominator).astype(BF)


def per_device(
    hidden,
    states,
    migration,
    routes,
    w_qkvz,
    w_ba,
    a_log,
    dt_bias,
    attn_gain,
    head_gain,
    w_out,
    moe_gain,
    w_router,
    w_gate_up,
    w_down,
):
    dp = ("x", "core")
    half = lax.axis_size("x")
    groups = half * lax.axis_size("core")
    members = lax.axis_size("expert")
    rows, width = hidden.shape
    depth = w_qkvz.shape[0]
    piece = width // members
    total_rows = routes.shape[0]
    leave_count = migration.shape[0] // groups
    plan = jnp.transpose(migration)
    shape = jax.ShapeDtypeStruct

    w_ba_t = jnp.transpose(w_ba)
    firsts = pl.pallas_call(
        functools.partial(first_kernel, groups, leave_count),
        out_shape=[pltpu.VMEM((depth, DK), BF)]
        + [pltpu.VMEM((rows * depth // LANES + DK, LANES), BF)] * (groups - 1)
        + [
            pltpu.VMEM((rows, DK, DV), F32),
            pltpu.VMEM(hidden.shape, BF),
            pltpu.VMEM(w_qkvz.shape, BF),
            pltpu.VMEM(w_ba_t.shape, BF),
            pltpu.VMEM(hidden.shape, BF),
        ],
        in_specs=[HBM] * 6,
        out_specs=[VMEM] * (groups + 5),
        scratch_shapes=[
            pltpu.VMEM((1, width), F32),
            pltpu.SMEM(plan.shape, jnp.int32),
            pltpu.SemaphoreType.DMA,
            pltpu.SemaphoreType.DMA((6,)),
        ],
        compiler_params=PARAMS,
        cost_estimate=COST,
        name="first",
    )(*in_hbm(plan, states, hidden, w_qkvz, attn_gain.reshape(1, width), w_ba_t))
    held, hidden_near, w_near, w_ba_near, normed = firsts[groups:]
    other_qk = swap_with(firsts[0], "expert", 1)
    messages = [swap_with(firsts[i], dp, i) for i in range(1, groups)]
    operands = [w_out, head_gain.reshape(1, DV), moe_gain.reshape(1, width)]
    span = 2 * MOE_FF
    staged = pl.pallas_call(
        functools.partial(stage_kernel, groups),
        out_shape=[pltpu.VMEM(operand.shape, operand.dtype) for operand in operands]
        + [
            pltpu.VMEM((rows, piece), F32),
            pltpu.VMEM((1, piece), F32),
            pltpu.VMEM((total_rows // 2, LANES), F32),
            pltpu.VMEM((width + width // span * MOE_FF + 16, span), BF),
        ],
        in_specs=[VMEM] * 4 + [HBM] * (2 + len(operands)),
        out_specs=[VMEM] * (4 + len(operands)),
        scratch_shapes=[pltpu.SemaphoreType.DMA((1 + width // span + len(operands),))],
        compiler_params=PARAMS,
        cost_estimate=COST,
        name="stage",
    )(
        hidden_near,
        *in_hbm(moe_gain.reshape(1, width), jnp.transpose(routes), jnp.transpose(w_router)),
        *in_hbm(w_gate_up, w_down, *operands),
    )
    w_out_near, head_gain_near, moe_gain_near = staged[:-4]
    own_hidden, own_gain, hits, expert = staged[-4:]

    partials = pl.pallas_call(
        functools.partial(project_kernel, groups),
        out_shape=[pltpu.VMEM((rows, SENT), F32)] * groups,
        in_specs=[VMEM] * 4 + [ANY] + [VMEM] * (groups - 1),
        out_specs=[VMEM] * groups,
        scratch_shapes=[pltpu.VMEM((total_rows, depth), BF)],
        compiler_params=PARAMS,
        cost_estimate=COST,
        name="project",
    )(normed, w_ba_near, w_near, other_qk, own_gain, *messages)
    after = partials[0]
    partials = [partials[0]] + [swap_with(partials[i], dp, i) for i in range(1, groups)]
    held, mixing = pl.pallas_call(
        functools.partial(settle_kernel, groups, leave_count),
        out_shape=[pltpu.VMEM((rows, DK, DV), F32), pltpu.VMEM((2, LANES), F32)],
        in_specs=[HBM] + [SMEM] * 2 + [VMEM, ANY] + [VMEM] * (groups - 1),
        out_specs=[VMEM] * 2,
        scratch_shapes=[
            pltpu.VMEM((DK, DV), F32),
            pltpu.SMEM(plan.shape, jnp.int32),
            pltpu.SemaphoreType.DMA,
        ],
        input_output_aliases={3: 0},
        compiler_params=PARAMS,
        cost_estimate=COST,
        name="settle",
    )(*in_hbm(plan), a_log, dt_bias, held, after, *messages)

    attention, expert = pl.pallas_call(
        delta_kernel,
        out_shape=[
            pltpu.VMEM((members, rows, piece), BF),
            pltpu.VMEM(expert.shape, expert.dtype),
        ],
        in_specs=[VMEM] * 4 + [ANY] + [VMEM] * groups,
        out_specs=[VMEM, ANY],
        scratch_shapes=[pltpu.VMEM((rows, DV), F32)] * 2,
        input_output_aliases={4: 1},
        compiler_params=PARAMS,
        cost_estimate=COST,
        name="delta",
    )(mixing, head_gain_near, w_out_near, held, expert, *partials)
    other_expert = swap_with(expert, "core", 1)
    attention = lax.all_to_all(attention, "expert", split_axis=0, concat_axis=0, tiled=True)

    gained, residual = pl.pallas_call(
        residual_kernel,
        out_shape=[
            pltpu.VMEM((half * members, rows, piece), BF),
            pltpu.VMEM((rows, piece), F32),
        ],
        in_specs=[VMEM] * 3,
        out_specs=[VMEM] * 2,
        compiler_params=PARAMS,
        cost_estimate=COST,
        name="residual",
    )(attention, own_hidden, own_gain)
    every = lax.all_to_all(gained, ("x", "expert"), split_axis=0, concat_axis=0, tiled=True)

    height = rows * piece // LANES + 8
    sent = pl.pallas_call(
        functools.partial(expert_kernel, width),
        out_shape=pltpu.VMEM((half * members, height, LANES), BF),
        in_specs=[VMEM] * 5,
        out_specs=VMEM,
        compiler_params=PARAMS,
        cost_estimate=COST,
        name="experts",
    )(every, hits, moe_gain_near, expert, other_expert)
    back = lax.all_to_all(sent, ("x", "expert"), split_axis=0, concat_axis=0, tiled=True)
    return pl.pallas_call(
        final_kernel,
        out_shape=shape((rows, piece), BF),
        in_specs=[VMEM] * 2,
        out_specs=VMEM,
        compiler_params=PARAMS,
        cost_estimate=COST,
        name="finish",
    )(back, residual)


def solution(mesh):
    parts, groups, members = (mesh.shape[name] for name in ("parts", "dp", "expert"))
    devices = mesh.devices.reshape(parts, groups // 2, 2, members)
    fine = jax.sharding.Mesh(devices, ("parts", "x", "core", "expert"))
    placed = (
        P(("parts", "x", "core"), None),
        P(("parts", "x", "core"), "expert", None, None),
        P("parts", None),
        P("parts", None),
        P(("x", "core"), "expert"),
        P(("x", "core"), "expert"),
        P("expert"),
        P("expert"),
        P(),
        P(),
        P("expert", None),
        P(),
        P(None, ("x", "core", "expert")),
        P(("x", "core", "expert"), None, None),
        P(("x", "core", "expert"), None, None),
    )
    return jax.shard_map(
        per_device,
        mesh=fine,
        in_specs=placed,
        out_specs=P(("parts", "x", "core"), "expert"),
        check_vma=False,
    )
```

```python
import functools

import jax
import jax.numpy as jnp
from jax import lax
from jax.experimental import pallas as pl
from jax.experimental.pallas import tpu as pltpu
from jax.sharding import PartitionSpec as P

DK = 128
DV = 128
MOE_FF = 256
LANES = 128
SENT = 2 * DK + 2 * DV + LANES

EPS = 1e-06
BF = jnp.bfloat16
F32 = jnp.float32

VMEM = pl.BlockSpec(memory_space=pltpu.VMEM)
SMEM = pl.BlockSpec(memory_space=pltpu.SMEM)
HBM = pl.BlockSpec(memory_space=pltpu.HBM)
ANY = pl.BlockSpec(memory_space=pl.ANY)
COST = pl.CostEstimate(flops=0, bytes_accessed=8 * 1024 * 1024, transcendentals=0)
PARAMS = pltpu.CompilerParams(vmem_limit_bytes=24 * 1024 * 1024)


def in_hbm(*values):
    return [pltpu.with_memory_space_constraint(value, pltpu.HBM) for value in values]


def copy_all(pairs, sems):
    copies = [pltpu.make_async_copy(a, b, sems.at[i]) for i, (a, b) in enumerate(pairs)]
    for copy in copies:
        copy.start()
    return copies


def swap_with(value, axis, offset):
    pairs = [(source, source ^ offset) for source in range(lax.axis_size(axis))]
    return lax.ppermute(value, axis, pairs)


def row_scale(values):
    return lax.rsqrt(jnp.mean(values * values, axis=-1, keepdims=True) + EPS)


def unit_rows(values):
    return values * lax.rsqrt(jnp.sum(values * values, axis=-1, keepdims=True) + EPS)


def group_index():
    return lax.axis_index("x") * lax.axis_size("core") + lax.axis_index("core")


def first_kernel(groups, leave_count, migration, states, hidden, w_qkvz, *refs):
    gain, w_ba, own_qk, messages = refs[0], refs[1], refs[2], refs[3 : groups + 2]
    held, hidden_near, w_near, w_ba_near, normed, gain_near, plan, plan_sem, sems = refs[groups + 2 :]
    plan_copy = pltpu.make_async_copy(migration, plan, plan_sem)
    plan_copy.start()
    pairs = [
        (hidden, hidden_near),
        (states.at[:, 0], held),
        (w_qkvz.at[:, pl.ds(0, DK)], own_qk),
        (w_qkvz, w_near),
        (gain, gain_near),
        (w_ba, w_ba_near),
    ]
    copies = copy_all(pairs, sems)
    group = group_index()
    rows = hidden.shape[0]
    depth = w_qkvz.shape[0]
    tiles = depth // LANES
    copies[0].wait()
    wide = hidden_near[...].astype(F32)
    copies[4].wait()
    normed[...] = (wide * row_scale(wide) * gain_near[...]).astype(BF)
    for i in range(1, groups):
        for c in range(tiles):
            first = pl.multiple_of((group ^ i) * depth + c * LANES, LANES)
            messages[i - 1][c * rows : (c + 1) * rows, :] = normed[:, pl.ds(first, LANES)]
    plan_copy.wait()
    copies[1].wait()
    for i in range(1, groups):
        slot = 0
        for j in range(leave_count):
            at = group * leave_count + j
            slot = jnp.where(plan[2, at] == (group ^ i), plan[1, at], slot)
        messages[i - 1][tiles * rows :, :] = held[slot].astype(BF)
    for copy in copies[2:4] + copies[5:]:
        copy.wait()


def project_kernel(groups, normed, w_ba, w_qkvz, *refs):
    messages, outs, scaled = refs[: groups - 1][::-1], refs[groups + 1 : -1], refs[-1]
    other_qk = refs[groups - 1]
    group = group_index()
    depth = w_qkvz.shape[0]
    rows = normed.shape[0]
    for c in range(depth // LANES):
        columns = pl.ds(pl.multiple_of(group * depth + c * LANES, LANES), LANES)
        for i in range(groups):
            part = normed[:, columns] if i == 0 else messages[i - 1][c * rows : (c + 1) * rows, :]
            scaled[i * rows : (i + 1) * rows, c * LANES : (c + 1) * LANES] = part
    x = scaled[...]
    main = jnp.dot(x, w_qkvz[...], preferred_element_type=F32)
    other = jnp.dot(x, other_qk[...], preferred_element_type=F32)
    wide = x.astype(F32)
    lane = lax.broadcasted_iota(jnp.int32, (groups * rows, LANES), 1)
    mixes = jnp.zeros((groups * rows, LANES), F32)
    for j in range(2):
        total = jnp.sum(wide * w_ba[j : j + 1, :].astype(F32), axis=1, keepdims=True)
        mixes = jnp.where(lane == j, total, mixes)
    for i in range(groups):
        block = slice(i * rows, (i + 1) * rows)
        outs[i][:, : DK + 2 * DV] = main[block]
        outs[i][:, DK + 2 * DV : 2 * DK + 2 * DV] = other[block]
        outs[i][:, 2 * DK + 2 * DV :] = mixes[block]


def stage_kernel(groups, hidden, gain, routes, router, w_gate_up, w_down, *refs):
    count = (len(refs) - 5) // 2
    sources, staged = refs[:count], refs[count : 2 * count]
    own_hidden, own_gain, hits, expert, sems = refs[-5:]
    width = hidden.shape[1]
    span = 2 * MOE_FF
    pairs = [(w_gate_up.at[0], expert.at[pl.ds(0, width)])]
    for c in range(width // span):
        pairs.append(
            (
                w_down.at[0, :, pl.ds(c * span, span)],
                expert.at[pl.ds(width + c * MOE_FF, MOE_FF)],
            )
        )
    copies = copy_all(list(zip(sources, staged)) + pairs, sems)
    line = lax.broadcasted_iota(jnp.int32, (16, span), 0)
    block = jnp.zeros((16, span), F32)
    for c in range(width // span):
        block = jnp.where(line == c, router[:, c * span : (c + 1) * span].astype(F32), block)
    expert[expert.shape[0] - 16 :, :] = block.astype(BF)
    group = group_index()
    core = lax.axis_index("core")
    member = lax.axis_index("expert")
    rows = hidden.shape[0]
    total_rows = groups * rows
    piece = own_hidden.shape[1]
    members = width // piece
    own, own_g = hidden[:, :piece], gain[:, :piece]
    for m in range(1, members):
        columns = slice(m * piece, (m + 1) * piece)
        own = jnp.where(member == m, hidden[:, columns], own)
        own_g = jnp.where(member == m, gain[:, columns], own_g)
    own_hidden[...] = own.astype(F32)
    own_gain[...] = own_g
    served = total_rows // 2
    row = lax.broadcasted_iota(jnp.int32, (served, total_rows), 0)
    lane = lax.broadcasted_iota(jnp.int32, (served, total_rows), 1)
    same = lane == (2 * (row // rows) + core) * rows + row % rows
    at = lax.broadcasted_iota(jnp.int32, hits.shape, 1)
    table = jnp.zeros(hits.shape, F32)
    for i in range(2):
        found = jnp.where(routes[...] == (group ^ i) * members + member, 1.0, 0.0)
        found = jnp.max(found, axis=0, keepdims=True)
        column = jnp.sum(jnp.where(same, found, 0.0), axis=1, keepdims=True)
        table = jnp.where(at == i, column, table)
    hits[...] = table
    for copy in copies:
        copy.wait()


def settle_kernel(groups, leave_count, migration, a_log, dt_bias, states, after, *refs):
    messages, (held, mixing, own_state, plan, plan_sem) = refs[:-5], refs[-5:]
    del after
    plan_copy = pltpu.make_async_copy(migration, plan, plan_sem)
    plan_copy.start()
    mixing[0:1, :] = jnp.exp(jnp.full((1, LANES), a_log[0], F32))
    mixing[1:2, :] = jnp.full((1, LANES), dt_bias[0], F32)
    group = group_index()
    plan_copy.wait()
    for j in range(leave_count):
        at = group * leave_count + j

        @pl.when(plan[2, at] == group)
        def _():
            own_state[...] = states[plan[1, at]]

    for i in range(groups):
        for j in range(leave_count):
            at = (group ^ i) * leave_count + j

            @pl.when(plan[2, at] == group)
            def _():
                if i == 0:
                    held[plan[3, at]] = own_state[...]
                else:
                    arrival = messages[i - 1]
                    held[plan[3, at]] = arrival[arrival.shape[0] - DK :, :].astype(F32)


def delta_kernel(mixing, head_gain, w_out, held, expert, *refs):
    partials, (out, passed, key_sums, query_sums) = refs[:-4], refs[-4:]
    del expert, passed
    member = lax.axis_index("expert")
    rows = held.shape[0]
    summed = partials[0][...]
    for partial in partials[1:]:
        summed = summed + partial[...]
    projected = summed.astype(BF).astype(F32)
    own_qk = projected[:, :DK]
    values = projected[:, DK : DK + DV]
    out_gate = projected[:, DK + DV : DK + 2 * DV]
    other = projected[:, DK + 2 * DV : 2 * DK + 2 * DV]
    write_mix = projected[:, 2 * DK + 2 * DV : 2 * DK + 2 * DV + 1]
    decay_mix = projected[:, 2 * DK + 2 * DV + 1 : 2 * DK + 2 * DV + 2]
    is_first = member % 2 == 0
    first = jnp.where(is_first, own_qk, other)
    second = jnp.where(is_first, other, own_qk)
    low_half = lax.broadcasted_iota(jnp.int32, (rows, DK), 1) < DK // 2
    queries = unit_rows(jnp.where(low_half, first, pltpu.roll(second, DK // 2, 1))) * DK ** (-0.5)
    keys_unit = unit_rows(jnp.where(low_half, pltpu.roll(first, DK // 2, 1), second))
    shifted = decay_mix + mixing[1:2, 0:1]
    soft = jnp.maximum(shifted, 0.0) + jnp.log1p(jnp.exp(-jnp.abs(shifted)))
    decay = jnp.exp(-mixing[0:1, 0:1] * soft)
    beta = jax.nn.sigmoid(write_mix)
    keys_t = jnp.transpose(keys_unit)
    queries_t = jnp.transpose(queries)
    for r in range(rows):
        state = held[r]
        key_sums[r : r + 1, :] = jnp.sum(state * keys_t[:, r : r + 1], axis=0, keepdims=True)
        query_sums[r : r + 1, :] = jnp.sum(state * queries_t[:, r : r + 1], axis=0, keepdims=True)
    correction = (values - key_sums[...] * decay) * beta
    overlap = jnp.sum(queries * keys_unit, axis=1, keepdims=True)
    readout = query_sums[...] * decay + overlap * correction
    normed = readout * row_scale(readout) * head_gain[...]
    gated = (normed * (out_gate * jax.nn.sigmoid(out_gate))).astype(BF)
    attention = jnp.dot(gated, w_out[...], preferred_element_type=F32).astype(BF)
    piece = out.shape[2]
    for m in range(out.shape[0]):
        out[m] = attention[:, m * piece : (m + 1) * piece]


def residual_kernel(attention, hidden, gain, gained, residual):
    members, rows, piece = attention.shape
    total = hidden[...]
    for m in range(members):
        total = total + attention[m].astype(F32)
    residual[...] = total
    sent = (total * gain[...]).astype(BF)
    for d in range(gained.shape[0]):
        gained[d] = sent


def packed(tile, piece):
    if piece >= LANES:
        return [tile[:, c : c + LANES] for c in range(0, piece, LANES)]
    count = LANES // piece
    part = tile.shape[0] // count
    return [jnp.concatenate([tile[c * part : (c + 1) * part] for c in range(count)], axis=1)]


def unpacked(tile, rows, piece):
    if piece >= LANES:
        return jnp.concatenate(
            [tile[c * rows : (c + 1) * rows] for c in range(piece // LANES)], axis=1
        )
    return jnp.concatenate([tile[:, c : c + piece] for c in range(0, LANES, piece)], axis=0)


def tail_of(weight):
    part = 8
    lane = lax.broadcasted_iota(jnp.int32, (part, LANES), 1)
    tail = jnp.zeros((part, LANES), F32)
    for c in range(weight.shape[0] // part):
        at = weight[c * part : (c + 1) * part]
        high = at.astype(BF).astype(F32)
        tail = jnp.where(lane == c, high, tail)
        tail = jnp.where(lane == LANES // 2 + c, at - high, tail)
    return tail


def expert_kernel(width, every, hits, gain, own, other, out):
    devices, rows, piece = every.shape
    members = width // piece
    half = devices // members
    total_rows = half * rows
    span = 2 * MOE_FF
    experts = (own, other)
    gate_up = [jnp.zeros((total_rows, span), F32)] * 2
    routed = [jnp.zeros((total_rows, piece), F32)] * 2
    squares = jnp.zeros((total_rows, piece), F32)
    inverse = 1.0 / gain[...]
    last = own.shape[0] - 16
    routers = [ref[last:, :].astype(F32) for ref in experts]
    for m in range(members):
        columns = slice(m * piece, (m + 1) * piece)
        line, first = m * piece // span, m * piece % span
        x = jnp.concatenate([every[g * members + m] for g in range(half)], axis=0)
        wide = x.astype(F32)
        plain = wide * inverse[:, columns]
        squares = squares + plain * plain
        for i in range(2):
            gate_up[i] = gate_up[i] + jnp.dot(x, experts[i][columns, :], preferred_element_type=F32)
            routed[i] = routed[i] + wide * routers[i][line : line + 1, first : first + piece]
    scale = lax.rsqrt(jnp.sum(squares, axis=1, keepdims=True) * (1.0 / width) + EPS)
    weights, acts = [], []
    for i in range(2):
        logits = jnp.sum(routed[i], axis=1, keepdims=True) * scale
        weights.append(jnp.where(hits[:, i : i + 1] > 0.0, jnp.exp(logits), 0.0))
        both = gate_up[i] * scale
        gate = both[:, :MOE_FF]
        acts.append((gate * jax.nn.sigmoid(gate) * both[:, MOE_FF:]).astype(BF))
    summed = weights[0] + weights[1]
    tails = [tail_of(summed[g * rows : (g + 1) * rows]) for g in range(half)]
    for c in range(width // span):
        down = slice(width + c * MOE_FF, width + (c + 1) * MOE_FF)
        y = jnp.zeros((total_rows, span), F32)
        for i in range(2):
            y = y + jnp.dot(acts[i], experts[i][down, :], preferred_element_type=F32) * weights[i]
        for m in range(span // piece):
            for g in range(half):
                tile = y[g * rows : (g + 1) * rows, m * piece : (m + 1) * piece]
                out[g * members + c * span // piece + m] = jnp.concatenate(
                    packed(tile, piece) + [tails[g]], axis=0
                ).astype(BF)


def final_kernel(back, residual, out):
    devices, height, _ = back.shape
    rows, piece = residual.shape
    total = back[0].astype(F32)
    for d in range(1, devices):
        total = total + back[d].astype(F32)
    body = rows * piece // LANES
    numerator = unpacked(total[:body], rows, piece)
    tail = total[body:]
    tail = tail + pltpu.roll(tail, LANES // 2, 1)
    denominator = jnp.concatenate(
        [tail[:, c : c + 1] for c in range(rows // tail.shape[0])], axis=0
    )
    out[...] = (residual[...] + numerator / denominator).astype(BF)


def per_device(
    hidden,
    states,
    migration,
    routes,
    w_qkvz,
    w_ba,
    a_log,
    dt_bias,
    attn_gain,
    head_gain,
    w_out,
    moe_gain,
    w_router,
    w_gate_up,
    w_down,
):
    dp = ("x", "core")
    half = lax.axis_size("x")
    groups = half * lax.axis_size("core")
    members = lax.axis_size("expert")
    rows, width = hidden.shape
    depth = w_qkvz.shape[0]
    piece = width // members
    total_rows = routes.shape[0]
    leave_count = migration.shape[0] // groups
    plan = jnp.transpose(migration)
    shape = jax.ShapeDtypeStruct

    w_ba_t = jnp.transpose(w_ba)
    firsts = pl.pallas_call(
        functools.partial(first_kernel, groups, leave_count),
        out_shape=[pltpu.VMEM((depth, DK), BF)]
        + [pltpu.VMEM((rows * depth // LANES + DK, LANES), BF)] * (groups - 1)
        + [
            pltpu.VMEM((rows, DK, DV), F32),
            pltpu.VMEM(hidden.shape, BF),
            pltpu.VMEM(w_qkvz.shape, BF),
            pltpu.VMEM(w_ba_t.shape, BF),
            pltpu.VMEM(hidden.shape, BF),
        ],
        in_specs=[HBM] * 6,
        out_specs=[VMEM] * (groups + 5),
        scratch_shapes=[
            pltpu.VMEM((1, width), F32),
            pltpu.SMEM(plan.shape, jnp.int32),
            pltpu.SemaphoreType.DMA,
            pltpu.SemaphoreType.DMA((6,)),
        ],
        compiler_params=PARAMS,
        cost_estimate=COST,
        name="first",
    )(*in_hbm(plan, states, hidden, w_qkvz, attn_gain.reshape(1, width), w_ba_t))
    held, hidden_near, w_near, w_ba_near, normed = firsts[groups:]
    other_qk = swap_with(firsts[0], "expert", 1)
    messages = [swap_with(firsts[i], dp, i) for i in range(1, groups)]
    operands = [w_out, head_gain.reshape(1, DV), moe_gain.reshape(1, width)]
    span = 2 * MOE_FF
    staged = pl.pallas_call(
        functools.partial(stage_kernel, groups),
        out_shape=[pltpu.VMEM(operand.shape, operand.dtype) for operand in operands]
        + [
            pltpu.VMEM((rows, piece), F32),
            pltpu.VMEM((1, piece), F32),
            pltpu.VMEM((total_rows // 2, LANES), F32),
            pltpu.VMEM((width + width // span * MOE_FF + 16, span), BF),
        ],
        in_specs=[VMEM] * 4 + [HBM] * (2 + len(operands)),
        out_specs=[VMEM] * (4 + len(operands)),
        scratch_shapes=[pltpu.SemaphoreType.DMA((1 + width // span + len(operands),))],
        compiler_params=PARAMS,
        cost_estimate=COST,
        name="stage",
    )(
        hidden_near,
        *in_hbm(moe_gain.reshape(1, width), jnp.transpose(routes), jnp.transpose(w_router)),
        *in_hbm(w_gate_up, w_down, *operands),
    )
    w_out_near, head_gain_near, moe_gain_near = staged[:-4]
    own_hidden, own_gain, hits, expert = staged[-4:]

    partials = pl.pallas_call(
        functools.partial(project_kernel, groups),
        out_shape=[pltpu.VMEM((rows, SENT), F32)] * groups,
        in_specs=[VMEM] * (3 + groups) + [ANY],
        out_specs=[VMEM] * groups,
        scratch_shapes=[pltpu.VMEM((total_rows, depth), BF)],
        compiler_params=PARAMS,
        cost_estimate=COST,
        name="project",
    )(normed, w_ba_near, w_near, *messages[::-1], other_qk, own_gain)
    after = partials[0]
    partials = [partials[0]] + [swap_with(partials[i], dp, i) for i in range(1, groups)]
    held, mixing = pl.pallas_call(
        functools.partial(settle_kernel, groups, leave_count),
        out_shape=[pltpu.VMEM((rows, DK, DV), F32), pltpu.VMEM((2, LANES), F32)],
        in_specs=[HBM] + [SMEM] * 2 + [VMEM, ANY] + [VMEM] * (groups - 1),
        out_specs=[VMEM] * 2,
        scratch_shapes=[
            pltpu.VMEM((DK, DV), F32),
            pltpu.SMEM(plan.shape, jnp.int32),
            pltpu.SemaphoreType.DMA,
        ],
        input_output_aliases={3: 0},
        compiler_params=PARAMS,
        cost_estimate=COST,
        name="settle",
    )(*in_hbm(plan), a_log, dt_bias, held, after, *messages)

    attention, expert = pl.pallas_call(
        delta_kernel,
        out_shape=[
            pltpu.VMEM((members, rows, piece), BF),
            pltpu.VMEM(expert.shape, expert.dtype),
        ],
        in_specs=[VMEM] * 4 + [ANY] + [VMEM] * groups,
        out_specs=[VMEM, ANY],
        scratch_shapes=[pltpu.VMEM((rows, DV), F32)] * 2,
        input_output_aliases={4: 1},
        compiler_params=PARAMS,
        cost_estimate=COST,
        name="delta",
    )(mixing, head_gain_near, w_out_near, held, expert, *partials[::-1])
    other_expert = swap_with(expert, "core", 1)
    attention = lax.all_to_all(attention, "expert", split_axis=0, concat_axis=0, tiled=True)

    gained, residual = pl.pallas_call(
        residual_kernel,
        out_shape=[
            pltpu.VMEM((half * members, rows, piece), BF),
            pltpu.VMEM((rows, piece), F32),
        ],
        in_specs=[VMEM] * 3,
        out_specs=[VMEM] * 2,
        compiler_params=PARAMS,
        cost_estimate=COST,
        name="residual",
    )(attention, own_hidden, own_gain)
    every = lax.all_to_all(gained, ("x", "expert"), split_axis=0, concat_axis=0, tiled=True)

    height = rows * piece // LANES + 8
    sent = pl.pallas_call(
        functools.partial(expert_kernel, width),
        out_shape=pltpu.VMEM((half * members, height, LANES), BF),
        in_specs=[VMEM] * 5,
        out_specs=VMEM,
        compiler_params=PARAMS,
        cost_estimate=COST,
        name="experts",
    )(every, hits, moe_gain_near, expert, other_expert)
    back = lax.all_to_all(sent, ("x", "expert"), split_axis=0, concat_axis=0, tiled=True)
    return pl.pallas_call(
        final_kernel,
        out_shape=shape((rows, piece), BF),
        in_specs=[VMEM] * 2,
        out_specs=VMEM,
        compiler_params=PARAMS,
        cost_estimate=COST,
        name="finish",
    )(back, residual)


def solution(mesh):
    parts, groups, members = (mesh.shape[name] for name in ("parts", "dp", "expert"))
    devices = mesh.devices.reshape(parts, groups // 2, 2, members)
    fine = jax.sharding.Mesh(devices, ("parts", "x", "core", "expert"))
    placed = (
        P(("parts", "x", "core"), None),
        P(("parts", "x", "core"), "expert", None, None),
        P("parts", None),
        P("parts", None),
        P(("x", "core"), "expert"),
        P(("x", "core"), "expert"),
        P("expert"),
        P("expert"),
        P(),
        P(),
        P("expert", None),
        P(),
        P(None, ("x", "core", "expert")),
        P(("x", "core", "expert"), None, None),
        P(("x", "core", "expert"), None, None),
    )
    return jax.shard_map(
        per_device,
        mesh=fine,
        in_specs=placed,
        out_specs=P(("parts", "x", "core"), "expert"),
        check_vma=False,
    )
```

```python
import functools

import jax
import jax.numpy as jnp
from jax import lax
from jax.experimental import pallas as pl
from jax.experimental.pallas import tpu as pltpu
from jax.sharding import PartitionSpec as P

DK = 128
DV = 128
MOE_FF = 256
LANES = 128
SENT = 2 * DK + 2 * DV + LANES

EPS = 1e-06
BF = jnp.bfloat16
F32 = jnp.float32

VMEM = pl.BlockSpec(memory_space=pltpu.VMEM)
SMEM = pl.BlockSpec(memory_space=pltpu.SMEM)
HBM = pl.BlockSpec(memory_space=pltpu.HBM)
ANY = pl.BlockSpec(memory_space=pl.ANY)
COST = pl.CostEstimate(flops=0, bytes_accessed=8 * 1024 * 1024, transcendentals=0)
PARAMS = pltpu.CompilerParams(vmem_limit_bytes=24 * 1024 * 1024)


def in_hbm(*values):
    return [pltpu.with_memory_space_constraint(value, pltpu.HBM) for value in values]


def copy_all(pairs, sems):
    copies = [pltpu.make_async_copy(a, b, sems.at[i]) for i, (a, b) in enumerate(pairs)]
    for copy in copies:
        copy.start()
    return copies


def swap_with(value, axis, offset):
    pairs = [(source, source ^ offset) for source in range(lax.axis_size(axis))]
    return lax.ppermute(value, axis, pairs)


def row_scale(values):
    return lax.rsqrt(jnp.mean(values * values, axis=-1, keepdims=True) + EPS)


def unit_rows(values):
    return values * lax.rsqrt(jnp.sum(values * values, axis=-1, keepdims=True) + EPS)


def group_index():
    return lax.axis_index("x") * lax.axis_size("core") + lax.axis_index("core")


def first_kernel(groups, leave_count, migration, states, hidden, w_qkvz, *refs):
    gain, w_ba, own_qk, messages = refs[0], refs[1], refs[2], refs[3 : groups + 2]
    held, hidden_near, w_near, w_ba_near, normed, gain_near, plan, plan_sem, sems = refs[groups + 2 :]
    plan_copy = pltpu.make_async_copy(migration, plan, plan_sem)
    plan_copy.start()
    pairs = [
        (hidden, hidden_near),
        (states.at[:, 0], held),
        (w_qkvz.at[:, pl.ds(0, DK)], own_qk),
        (w_qkvz, w_near),
        (gain, gain_near),
        (w_ba, w_ba_near),
    ]
    copies = copy_all(pairs, sems)
    group = group_index()
    rows = hidden.shape[0]
    depth = w_qkvz.shape[0]
    tiles = depth // LANES
    copies[0].wait()
    wide = hidden_near[...].astype(F32)
    copies[4].wait()
    normed[...] = (wide * row_scale(wide) * gain_near[...]).astype(BF)
    for i in range(1, groups):
        for c in range(tiles):
            first = pl.multiple_of((group ^ i) * depth + c * LANES, LANES)
            messages[i - 1][c * rows : (c + 1) * rows, :] = normed[:, pl.ds(first, LANES)]
    plan_copy.wait()
    copies[1].wait()
    for i in range(1, groups):
        slot = 0
        for j in range(leave_count):
            at = group * leave_count + j
            slot = jnp.where(plan[2, at] == (group ^ i), plan[1, at], slot)
        messages[i - 1][tiles * rows :, :] = held[slot].astype(BF)
    for copy in copies[2:4] + copies[5:]:
        copy.wait()


def project_kernel(groups, normed, w_ba, w_qkvz, *refs):
    messages, outs, scaled = refs[: groups - 1][::-1], refs[groups + 1 : -1], refs[-1]
    other_qk = refs[groups - 1]
    group = group_index()
    depth = w_qkvz.shape[0]
    rows = normed.shape[0]
    for c in range(depth // LANES):
        columns = pl.ds(pl.multiple_of(group * depth + c * LANES, LANES), LANES)
        for i in range(groups):
            part = normed[:, columns] if i == 0 else messages[i - 1][c * rows : (c + 1) * rows, :]
            scaled[i * rows : (i + 1) * rows, c * LANES : (c + 1) * LANES] = part
    x = scaled[...]
    main = jnp.dot(x, w_qkvz[...], preferred_element_type=F32)
    other = jnp.dot(x, other_qk[...], preferred_element_type=F32)
    wide = x.astype(F32)
    lane = lax.broadcasted_iota(jnp.int32, (groups * rows, LANES), 1)
    mixes = jnp.zeros((groups * rows, LANES), F32)
    for j in range(2):
        total = jnp.sum(wide * w_ba[j : j + 1, :].astype(F32), axis=1, keepdims=True)
        mixes = jnp.where(lane == j, total, mixes)
    for i in range(groups):
        block = slice(i * rows, (i + 1) * rows)
        outs[i][:, : DK + 2 * DV] = main[block]
        outs[i][:, DK + 2 * DV : 2 * DK + 2 * DV] = other[block]
        outs[i][:, 2 * DK + 2 * DV :] = mixes[block]


def stage_kernel(groups, hidden, gain, routes, router, w_gate_up, w_down, *refs):
    count = (len(refs) - 5) // 2
    sources, staged = refs[:count], refs[count : 2 * count]
    own_hidden, own_gain, hits, expert, sems = refs[-5:]
    width = hidden.shape[1]
    span = 2 * MOE_FF
    pairs = [(w_gate_up.at[0], expert.at[pl.ds(0, width)])]
    for c in range(width // span):
        pairs.append(
            (
                w_down.at[0, :, pl.ds(c * span, span)],
                expert.at[pl.ds(width + c * MOE_FF, MOE_FF)],
            )
        )
    copies = copy_all(list(zip(sources, staged)) + pairs, sems)
    line = lax.broadcasted_iota(jnp.int32, (16, span), 0)
    block = jnp.zeros((16, span), F32)
    for c in range(width // span):
        block = jnp.where(line == c, router[:, c * span : (c + 1) * span].astype(F32), block)
    expert[expert.shape[0] - 16 :, :] = block.astype(BF)
    group = group_index()
    core = lax.axis_index("core")
    member = lax.axis_index("expert")
    rows = hidden.shape[0]
    total_rows = groups * rows
    piece = own_hidden.shape[1]
    members = width // piece
    own, own_g = hidden[:, :piece], gain[:, :piece]
    for m in range(1, members):
        columns = slice(m * piece, (m + 1) * piece)
        own = jnp.where(member == m, hidden[:, columns], own)
        own_g = jnp.where(member == m, gain[:, columns], own_g)
    own_hidden[...] = own.astype(F32)
    own_gain[...] = own_g
    served = total_rows // 2
    row = lax.broadcasted_iota(jnp.int32, (served, total_rows), 0)
    lane = lax.broadcasted_iota(jnp.int32, (served, total_rows), 1)
    same = lane == (2 * (row // rows) + core) * rows + row % rows
    at = lax.broadcasted_iota(jnp.int32, hits.shape, 1)
    table = jnp.zeros(hits.shape, F32)
    for i in range(2):
        found = jnp.where(routes[...] == (group ^ i) * members + member, 1.0, 0.0)
        found = jnp.max(found, axis=0, keepdims=True)
        column = jnp.sum(jnp.where(same, found, 0.0), axis=1, keepdims=True)
        table = jnp.where(at == i, column, table)
    hits[...] = table
    for copy in copies:
        copy.wait()


def store_split(out, row, state):
    high = state.astype(BF)
    where = pl.ds(pl.multiple_of(row * DK, DK), DK)
    out[where, :DV] = high
    out[where, DV:] = (state - high.astype(F32)).astype(BF)


def settle_kernel(groups, leave_count, migration, a_log, dt_bias, states, after, *refs):
    messages, (split, mixing, plan, plan_sem) = refs[:-4], refs[-4:]
    del after
    plan_copy = pltpu.make_async_copy(migration, plan, plan_sem)
    plan_copy.start()
    mixing[0:1, :] = jnp.exp(jnp.full((1, LANES), a_log[0], F32))
    mixing[1:2, :] = jnp.full((1, LANES), dt_bias[0], F32)
    group = group_index()
    for r in range(states.shape[0]):
        store_split(split, r, states[r])
    plan_copy.wait()
    for i in range(groups):
        for j in range(leave_count):
            at = (group ^ i) * leave_count + j

            @pl.when(plan[2, at] == group)
            def _():
                if i == 0:
                    state = states[plan[1, at]]
                else:
                    arrival = messages[i - 1]
                    state = arrival[arrival.shape[0] - DK :, :].astype(F32)
                store_split(split, plan[3, at], state)


def delta_kernel(mixing, head_gain, w_out, split, expert, *refs):
    partials, (out, passed, blocks) = refs[:-3], refs[-3:]
    del expert, passed
    member = lax.axis_index("expert")
    rows = split.shape[0] // DK
    summed = partials[0][...]
    for partial in partials[1:]:
        summed = summed + partial[...]
    projected = summed.astype(BF).astype(F32)
    own_qk = projected[:, :DK]
    values = projected[:, DK : DK + DV]
    out_gate = projected[:, DK + DV : DK + 2 * DV]
    other = projected[:, DK + 2 * DV : 2 * DK + 2 * DV]
    write_mix = projected[:, 2 * DK + 2 * DV : 2 * DK + 2 * DV + 1]
    decay_mix = projected[:, 2 * DK + 2 * DV + 1 : 2 * DK + 2 * DV + 2]
    is_first = member % 2 == 0
    first = jnp.where(is_first, own_qk, other)
    second = jnp.where(is_first, other, own_qk)
    low_half = lax.broadcasted_iota(jnp.int32, (rows, DK), 1) < DK // 2
    queries = unit_rows(jnp.where(low_half, first, pltpu.roll(second, DK // 2, 1))) * DK ** (-0.5)
    keys_unit = unit_rows(jnp.where(low_half, pltpu.roll(first, DK // 2, 1), second))
    shifted = decay_mix + mixing[1:2, 0:1]
    soft = jnp.maximum(shifted, 0.0) + jnp.log1p(jnp.exp(-jnp.abs(shifted)))
    decay = jnp.exp(-mixing[0:1, 0:1] * soft)
    beta = jax.nn.sigmoid(write_mix)
    both = jnp.concatenate([keys_unit, queries], axis=0)
    high = both.astype(BF).astype(F32)
    both = jnp.concatenate([high, both - high], axis=0)
    row = lax.broadcasted_iota(jnp.int32, both.shape, 0) % rows
    for r in range(rows):
        blocks[:, r * DK : (r + 1) * DK] = jnp.where(row == r, both, 0.0).astype(BF)
    sums = jnp.dot(blocks[...], split[...], preferred_element_type=F32)
    sums = sums[:, :DV] + sums[:, DV:]
    sums = sums[: 2 * rows] + sums[2 * rows :]
    key_sums, query_sums = sums[:rows], sums[rows:]
    correction = (values - key_sums * decay) * beta
    overlap = jnp.sum(queries * keys_unit, axis=1, keepdims=True)
    readout = query_sums * decay + overlap * correction
    normed = readout * row_scale(readout) * head_gain[...]
    gated = (normed * (out_gate * jax.nn.sigmoid(out_gate))).astype(BF)
    attention = jnp.dot(gated, w_out[...], preferred_element_type=F32).astype(BF)
    piece = out.shape[2]
    for m in range(out.shape[0]):
        out[m] = attention[:, m * piece : (m + 1) * piece]


def residual_kernel(attention, hidden, gain, gained, residual):
    members, rows, piece = attention.shape
    total = hidden[...]
    for m in range(members):
        total = total + attention[m].astype(F32)
    residual[...] = total
    sent = (total * gain[...]).astype(BF)
    for d in range(gained.shape[0]):
        gained[d] = sent


def packed(tile, piece):
    if piece >= LANES:
        return [tile[:, c : c + LANES] for c in range(0, piece, LANES)]
    count = LANES // piece
    part = tile.shape[0] // count
    return [jnp.concatenate([tile[c * part : (c + 1) * part] for c in range(count)], axis=1)]


def unpacked(tile, rows, piece):
    if piece >= LANES:
        return jnp.concatenate(
            [tile[c * rows : (c + 1) * rows] for c in range(piece // LANES)], axis=1
        )
    return jnp.concatenate([tile[:, c : c + piece] for c in range(0, LANES, piece)], axis=0)


def tail_of(weight):
    part = 8
    lane = lax.broadcasted_iota(jnp.int32, (part, LANES), 1)
    tail = jnp.zeros((part, LANES), F32)
    for c in range(weight.shape[0] // part):
        at = weight[c * part : (c + 1) * part]
        high = at.astype(BF).astype(F32)
        tail = jnp.where(lane == c, high, tail)
        tail = jnp.where(lane == LANES // 2 + c, at - high, tail)
    return tail


def expert_kernel(width, every, hits, gain, own, other, out):
    devices, rows, piece = every.shape
    members = width // piece
    half = devices // members
    total_rows = half * rows
    span = 2 * MOE_FF
    experts = (own, other)
    gate_up = [jnp.zeros((total_rows, span), F32)] * 2
    routed = [jnp.zeros((total_rows, piece), F32)] * 2
    squares = jnp.zeros((total_rows, piece), F32)
    inverse = 1.0 / gain[...]
    last = own.shape[0] - 16
    routers = [ref[last:, :].astype(F32) for ref in experts]
    for m in range(members):
        columns = slice(m * piece, (m + 1) * piece)
        line, first = m * piece // span, m * piece % span
        x = jnp.concatenate([every[g * members + m] for g in range(half)], axis=0)
        wide = x.astype(F32)
        plain = wide * inverse[:, columns]
        squares = squares + plain * plain
        for i in range(2):
            gate_up[i] = gate_up[i] + jnp.dot(x, experts[i][columns, :], preferred_element_type=F32)
            routed[i] = routed[i] + wide * routers[i][line : line + 1, first : first + piece]
    scale = lax.rsqrt(jnp.sum(squares, axis=1, keepdims=True) * (1.0 / width) + EPS)
    weights, acts = [], []
    for i in range(2):
        logits = jnp.sum(routed[i], axis=1, keepdims=True) * scale
        weights.append(jnp.where(hits[:, i : i + 1] > 0.0, jnp.exp(logits), 0.0))
        both = gate_up[i] * scale
        gate = both[:, :MOE_FF]
        acts.append((gate * jax.nn.sigmoid(gate) * both[:, MOE_FF:]).astype(BF))
    summed = weights[0] + weights[1]
    tails = [tail_of(summed[g * rows : (g + 1) * rows]) for g in range(half)]
    for c in range(width // span):
        down = slice(width + c * MOE_FF, width + (c + 1) * MOE_FF)
        y = jnp.zeros((total_rows, span), F32)
        for i in range(2):
            y = y + jnp.dot(acts[i], experts[i][down, :], preferred_element_type=F32) * weights[i]
        for m in range(span // piece):
            for g in range(half):
                tile = y[g * rows : (g + 1) * rows, m * piece : (m + 1) * piece]
                out[g * members + c * span // piece + m] = jnp.concatenate(
                    packed(tile, piece) + [tails[g]], axis=0
                ).astype(BF)


def final_kernel(back, residual, out):
    devices, height, _ = back.shape
    rows, piece = residual.shape
    total = back[0].astype(F32)
    for d in range(1, devices):
        total = total + back[d].astype(F32)
    body = rows * piece // LANES
    numerator = unpacked(total[:body], rows, piece)
    tail = total[body:]
    tail = tail + pltpu.roll(tail, LANES // 2, 1)
    denominator = jnp.concatenate(
        [tail[:, c : c + 1] for c in range(rows // tail.shape[0])], axis=0
    )
    out[...] = (residual[...] + numerator / denominator).astype(BF)


def per_device(
    hidden,
    states,
    migration,
    routes,
    w_qkvz,
    w_ba,
    a_log,
    dt_bias,
    attn_gain,
    head_gain,
    w_out,
    moe_gain,
    w_router,
    w_gate_up,
    w_down,
):
    dp = ("x", "core")
    half = lax.axis_size("x")
    groups = half * lax.axis_size("core")
    members = lax.axis_size("expert")
    rows, width = hidden.shape
    depth = w_qkvz.shape[0]
    piece = width // members
    total_rows = routes.shape[0]
    leave_count = migration.shape[0] // groups
    plan = jnp.transpose(migration)
    shape = jax.ShapeDtypeStruct

    w_ba_t = jnp.transpose(w_ba)
    firsts = pl.pallas_call(
        functools.partial(first_kernel, groups, leave_count),
        out_shape=[pltpu.VMEM((depth, DK), BF)]
        + [pltpu.VMEM((rows * depth // LANES + DK, LANES), BF)] * (groups - 1)
        + [
            pltpu.VMEM((rows, DK, DV), F32),
            pltpu.VMEM(hidden.shape, BF),
            pltpu.VMEM(w_qkvz.shape, BF),
            pltpu.VMEM(w_ba_t.shape, BF),
            pltpu.VMEM(hidden.shape, BF),
        ],
        in_specs=[HBM] * 6,
        out_specs=[VMEM] * (groups + 5),
        scratch_shapes=[
            pltpu.VMEM((1, width), F32),
            pltpu.SMEM(plan.shape, jnp.int32),
            pltpu.SemaphoreType.DMA,
            pltpu.SemaphoreType.DMA((6,)),
        ],
        compiler_params=PARAMS,
        cost_estimate=COST,
        name="first",
    )(*in_hbm(plan, states, hidden, w_qkvz, attn_gain.reshape(1, width), w_ba_t))
    held, hidden_near, w_near, w_ba_near, normed = firsts[groups:]
    other_qk = swap_with(firsts[0], "expert", 1)
    messages = [swap_with(firsts[i], dp, i) for i in range(1, groups)]
    operands = [w_out, head_gain.reshape(1, DV), moe_gain.reshape(1, width)]
    span = 2 * MOE_FF
    staged = pl.pallas_call(
        functools.partial(stage_kernel, groups),
        out_shape=[pltpu.VMEM(operand.shape, operand.dtype) for operand in operands]
        + [
            pltpu.VMEM((rows, piece), F32),
            pltpu.VMEM((1, piece), F32),
            pltpu.VMEM((total_rows // 2, LANES), F32),
            pltpu.VMEM((width + width // span * MOE_FF + 16, span), BF),
        ],
        in_specs=[VMEM] * 4 + [HBM] * (2 + len(operands)),
        out_specs=[VMEM] * (4 + len(operands)),
        scratch_shapes=[pltpu.SemaphoreType.DMA((1 + width // span + len(operands),))],
        compiler_params=PARAMS,
        cost_estimate=COST,
        name="stage",
    )(
        hidden_near,
        *in_hbm(moe_gain.reshape(1, width), jnp.transpose(routes), jnp.transpose(w_router)),
        *in_hbm(w_gate_up, w_down, *operands),
    )
    w_out_near, head_gain_near, moe_gain_near = staged[:-4]
    own_hidden, own_gain, hits, expert = staged[-4:]

    partials = pl.pallas_call(
        functools.partial(project_kernel, groups),
        out_shape=[pltpu.VMEM((rows, SENT), F32)] * groups,
        in_specs=[VMEM] * (3 + groups) + [ANY],
        out_specs=[VMEM] * groups,
        scratch_shapes=[pltpu.VMEM((total_rows, depth), BF)],
        compiler_params=PARAMS,
        cost_estimate=COST,
        name="project",
    )(normed, w_ba_near, w_near, *messages[::-1], other_qk, own_gain)
    after = partials[0]
    partials = [partials[0]] + [swap_with(partials[i], dp, i) for i in range(1, groups)]
    split, mixing = pl.pallas_call(
        functools.partial(settle_kernel, groups, leave_count),
        out_shape=[pltpu.VMEM((rows * DK, 2 * DV), BF), pltpu.VMEM((2, LANES), F32)],
        in_specs=[HBM] + [SMEM] * 2 + [VMEM, ANY] + [VMEM] * (groups - 1),
        out_specs=[VMEM] * 2,
        scratch_shapes=[pltpu.SMEM(plan.shape, jnp.int32), pltpu.SemaphoreType.DMA],
        compiler_params=PARAMS,
        cost_estimate=COST,
        name="settle",
    )(*in_hbm(plan), a_log, dt_bias, held, after, *messages)

    attention, expert = pl.pallas_call(
        delta_kernel,
        out_shape=[
            pltpu.VMEM((members, rows, piece), BF),
            pltpu.VMEM(expert.shape, expert.dtype),
        ],
        in_specs=[VMEM] * 4 + [ANY] + [VMEM] * groups,
        out_specs=[VMEM, ANY],
        scratch_shapes=[pltpu.VMEM((4 * rows, rows * DK), BF)],
        input_output_aliases={4: 1},
        compiler_params=PARAMS,
        cost_estimate=COST,
        name="delta",
    )(mixing, head_gain_near, w_out_near, split, expert, *partials[::-1])
    other_expert = swap_with(expert, "core", 1)
    attention = lax.all_to_all(attention, "expert", split_axis=0, concat_axis=0, tiled=True)

    gained, residual = pl.pallas_call(
        residual_kernel,
        out_shape=[
            pltpu.VMEM((half * members, rows, piece), BF),
            pltpu.VMEM((rows, piece), F32),
        ],
        in_specs=[VMEM] * 3,
        out_specs=[VMEM] * 2,
        compiler_params=PARAMS,
        cost_estimate=COST,
        name="residual",
    )(attention, own_hidden, own_gain)
    every = lax.all_to_all(gained, ("x", "expert"), split_axis=0, concat_axis=0, tiled=True)

    height = rows * piece // LANES + 8
    sent = pl.pallas_call(
        functools.partial(expert_kernel, width),
        out_shape=pltpu.VMEM((half * members, height, LANES), BF),
        in_specs=[VMEM] * 5,
        out_specs=VMEM,
        compiler_params=PARAMS,
        cost_estimate=COST,
        name="experts",
    )(every, hits, moe_gain_near, expert, other_expert)
    back = lax.all_to_all(sent, ("x", "expert"), split_axis=0, concat_axis=0, tiled=True)
    return pl.pallas_call(
        final_kernel,
        out_shape=shape((rows, piece), BF),
        in_specs=[VMEM] * 2,
        out_specs=VMEM,
        compiler_params=PARAMS,
        cost_estimate=COST,
        name="finish",
    )(back, residual)


def solution(mesh):
    parts, groups, members = (mesh.shape[name] for name in ("parts", "dp", "expert"))
    devices = mesh.devices.reshape(parts, groups // 2, 2, members)
    fine = jax.sharding.Mesh(devices, ("parts", "x", "core", "expert"))
    placed = (
        P(("parts", "x", "core"), None),
        P(("parts", "x", "core"), "expert", None, None),
        P("parts", None),
        P("parts", None),
        P(("x", "core"), "expert"),
        P(("x", "core"), "expert"),
        P("expert"),
        P("expert"),
        P(),
        P(),
        P("expert", None),
        P(),
        P(None, ("x", "core", "expert")),
        P(("x", "core", "expert"), None, None),
        P(("x", "core", "expert"), None, None),
    )
    return jax.shard_map(
        per_device,
        mesh=fine,
        in_specs=placed,
        out_specs=P(("parts", "x", "core"), "expert"),
        check_vma=False,
    )
```

```python
import functools

import jax
import jax.numpy as jnp
from jax import lax
from jax.experimental import pallas as pl
from jax.experimental.pallas import tpu as pltpu
from jax.sharding import PartitionSpec as P

DK = 128
DV = 128
MOE_FF = 256
LANES = 128
SENT = 2 * DK + 2 * DV + LANES

EPS = 1e-06
BF = jnp.bfloat16
F32 = jnp.float32

VMEM = pl.BlockSpec(memory_space=pltpu.VMEM)
SMEM = pl.BlockSpec(memory_space=pltpu.SMEM)
HBM = pl.BlockSpec(memory_space=pltpu.HBM)
ANY = pl.BlockSpec(memory_space=pl.ANY)
COST = pl.CostEstimate(flops=0, bytes_accessed=8 * 1024 * 1024, transcendentals=0)
PARAMS = pltpu.CompilerParams(vmem_limit_bytes=24 * 1024 * 1024)


def in_hbm(*values):
    return [pltpu.with_memory_space_constraint(value, pltpu.HBM) for value in values]


def copy_all(pairs, sems):
    copies = [pltpu.make_async_copy(a, b, sems.at[i]) for i, (a, b) in enumerate(pairs)]
    for copy in copies:
        copy.start()
    return copies


def swap_with(value, axis, offset):
    pairs = [(source, source ^ offset) for source in range(lax.axis_size(axis))]
    return lax.ppermute(value, axis, pairs)


def row_scale(values):
    return lax.rsqrt(jnp.mean(values * values, axis=-1, keepdims=True) + EPS)


def unit_rows(values):
    return values * lax.rsqrt(jnp.sum(values * values, axis=-1, keepdims=True) + EPS)


def group_index():
    return lax.axis_index("x") * lax.axis_size("core") + lax.axis_index("core")


def first_kernel(groups, leave_count, migration, states, hidden, w_qkvz, *refs):
    gain, w_ba, own_qk, messages = refs[0], refs[1], refs[2], refs[3 : groups + 2]
    held, hidden_near, w_ba_near, normed, gain_near, plan, plan_sem, sems = refs[groups + 2 :]
    plan_copy = pltpu.make_async_copy(migration, plan, plan_sem)
    plan_copy.start()
    pairs = [
        (hidden, hidden_near),
        (states.at[:, 0], held),
        (w_qkvz.at[:, pl.ds(0, DK)], own_qk),
        (gain, gain_near),
        (w_ba, w_ba_near),
    ]
    copies = copy_all(pairs, sems)
    group = group_index()
    rows = hidden.shape[0]
    depth = w_qkvz.shape[0]
    tiles = depth // LANES
    copies[0].wait()
    wide = hidden_near[...].astype(F32)
    copies[3].wait()
    normed[...] = (wide * row_scale(wide) * gain_near[...]).astype(BF)
    for i in range(1, groups):
        for c in range(tiles):
            first = pl.multiple_of((group ^ i) * depth + c * LANES, LANES)
            messages[i - 1][c * rows : (c + 1) * rows, :] = normed[:, pl.ds(first, LANES)]
    plan_copy.wait()
    copies[1].wait()
    for i in range(1, groups):
        slot = 0
        for j in range(leave_count):
            at = group * leave_count + j
            slot = jnp.where(plan[2, at] == (group ^ i), plan[1, at], slot)
        messages[i - 1][tiles * rows :, :] = held[slot].astype(BF)
    for copy in copies[2:3] + copies[4:]:
        copy.wait()


def project_kernel(groups, normed, w_ba, w_qkvz, *refs):
    messages, outs, scaled = refs[: groups - 1][::-1], refs[groups + 1 : -1], refs[-1]
    other_qk = refs[groups - 1]
    group = group_index()
    depth = w_qkvz.shape[0]
    rows = normed.shape[0]
    for c in range(depth // LANES):
        columns = pl.ds(pl.multiple_of(group * depth + c * LANES, LANES), LANES)
        for i in range(groups):
            part = normed[:, columns] if i == 0 else messages[i - 1][c * rows : (c + 1) * rows, :]
            scaled[i * rows : (i + 1) * rows, c * LANES : (c + 1) * LANES] = part
    x = scaled[...]
    main = jnp.dot(x, w_qkvz[...], preferred_element_type=F32)
    other = jnp.dot(x, other_qk[...], preferred_element_type=F32)
    wide = x.astype(F32)
    lane = lax.broadcasted_iota(jnp.int32, (groups * rows, LANES), 1)
    mixes = jnp.zeros((groups * rows, LANES), F32)
    for j in range(2):
        total = jnp.sum(wide * w_ba[j : j + 1, :].astype(F32), axis=1, keepdims=True)
        mixes = jnp.where(lane == j, total, mixes)
    for i in range(groups):
        block = slice(i * rows, (i + 1) * rows)
        outs[i][:, : DK + 2 * DV] = main[block]
        outs[i][:, DK + 2 * DV : 2 * DK + 2 * DV] = other[block]
        outs[i][:, 2 * DK + 2 * DV :] = mixes[block]


def stage_kernel(groups, hidden, gain, routes, router, w_gate_up, w_down, *refs):
    count = (len(refs) - 5) // 2
    sources, staged = refs[:count], refs[count : 2 * count]
    own_hidden, own_gain, hits, expert, sems = refs[-5:]
    width = hidden.shape[1]
    span = 2 * MOE_FF
    pairs = [(w_gate_up.at[0], expert.at[pl.ds(0, width)])]
    for c in range(width // span):
        pairs.append(
            (
                w_down.at[0, :, pl.ds(c * span, span)],
                expert.at[pl.ds(width + c * MOE_FF, MOE_FF)],
            )
        )
    copies = copy_all(list(zip(sources, staged)) + pairs, sems)
    line = lax.broadcasted_iota(jnp.int32, (16, span), 0)
    block = jnp.zeros((16, span), F32)
    for c in range(width // span):
        block = jnp.where(line == c, router[:, c * span : (c + 1) * span].astype(F32), block)
    expert[expert.shape[0] - 16 :, :] = block.astype(BF)
    group = group_index()
    core = lax.axis_index("core")
    member = lax.axis_index("expert")
    rows = hidden.shape[0]
    total_rows = groups * rows
    piece = own_hidden.shape[1]
    members = width // piece
    own, own_g = hidden[:, :piece], gain[:, :piece]
    for m in range(1, members):
        columns = slice(m * piece, (m + 1) * piece)
        own = jnp.where(member == m, hidden[:, columns], own)
        own_g = jnp.where(member == m, gain[:, columns], own_g)
    own_hidden[...] = own.astype(F32)
    own_gain[...] = own_g
    served = total_rows // 2
    row = lax.broadcasted_iota(jnp.int32, (served, total_rows), 0)
    lane = lax.broadcasted_iota(jnp.int32, (served, total_rows), 1)
    same = lane == (2 * (row // rows) + core) * rows + row % rows
    at = lax.broadcasted_iota(jnp.int32, hits.shape, 1)
    table = jnp.zeros(hits.shape, F32)
    for i in range(2):
        found = jnp.where(routes[...] == (group ^ i) * members + member, 1.0, 0.0)
        found = jnp.max(found, axis=0, keepdims=True)
        column = jnp.sum(jnp.where(same, found, 0.0), axis=1, keepdims=True)
        table = jnp.where(at == i, column, table)
    hits[...] = table
    for copy in copies:
        copy.wait()


def store_split(out, row, state):
    high = state.astype(BF)
    where = pl.ds(pl.multiple_of(row * DK, DK), DK)
    out[where, :DV] = high
    out[where, DV:] = (state - high.astype(F32)).astype(BF)


def settle_kernel(groups, leave_count, migration, a_log, dt_bias, states, after, *refs):
    messages, (split, mixing, plan, plan_sem) = refs[:-4], refs[-4:]
    del after
    plan_copy = pltpu.make_async_copy(migration, plan, plan_sem)
    plan_copy.start()
    mixing[0:1, :] = jnp.exp(jnp.full((1, LANES), a_log[0], F32))
    mixing[1:2, :] = jnp.full((1, LANES), dt_bias[0], F32)
    group = group_index()
    for r in range(states.shape[0]):
        store_split(split, r, states[r])
    plan_copy.wait()
    for i in range(groups):
        for j in range(leave_count):
            at = (group ^ i) * leave_count + j

            @pl.when(plan[2, at] == group)
            def _():
                if i == 0:
                    state = states[plan[1, at]]
                else:
                    arrival = messages[i - 1]
                    state = arrival[arrival.shape[0] - DK :, :].astype(F32)
                store_split(split, plan[3, at], state)


def delta_kernel(mixing, head_gain, w_out, split, expert, *refs):
    partials, (out, passed, blocks) = refs[:-3], refs[-3:]
    del expert, passed
    member = lax.axis_index("expert")
    rows = split.shape[0] // DK
    summed = partials[0][...]
    for partial in partials[1:]:
        summed = summed + partial[...]
    projected = summed.astype(BF).astype(F32)
    own_qk = projected[:, :DK]
    values = projected[:, DK : DK + DV]
    out_gate = projected[:, DK + DV : DK + 2 * DV]
    other = projected[:, DK + 2 * DV : 2 * DK + 2 * DV]
    write_mix = projected[:, 2 * DK + 2 * DV : 2 * DK + 2 * DV + 1]
    decay_mix = projected[:, 2 * DK + 2 * DV + 1 : 2 * DK + 2 * DV + 2]
    is_first = member % 2 == 0
    first = jnp.where(is_first, own_qk, other)
    second = jnp.where(is_first, other, own_qk)
    low_half = lax.broadcasted_iota(jnp.int32, (rows, DK), 1) < DK // 2
    queries = unit_rows(jnp.where(low_half, first, pltpu.roll(second, DK // 2, 1))) * DK ** (-0.5)
    keys_unit = unit_rows(jnp.where(low_half, pltpu.roll(first, DK // 2, 1), second))
    shifted = decay_mix + mixing[1:2, 0:1]
    soft = jnp.maximum(shifted, 0.0) + jnp.log1p(jnp.exp(-jnp.abs(shifted)))
    decay = jnp.exp(-mixing[0:1, 0:1] * soft)
    beta = jax.nn.sigmoid(write_mix)
    both = jnp.concatenate([keys_unit, queries], axis=0)
    high = both.astype(BF).astype(F32)
    both = jnp.concatenate([high, both - high], axis=0)
    row = lax.broadcasted_iota(jnp.int32, both.shape, 0) % rows
    for r in range(rows):
        blocks[:, r * DK : (r + 1) * DK] = jnp.where(row == r, both, 0.0).astype(BF)
    sums = jnp.dot(blocks[...], split[...], preferred_element_type=F32)
    sums = sums[:, :DV] + sums[:, DV:]
    sums = sums[: 2 * rows] + sums[2 * rows :]
    key_sums, query_sums = sums[:rows], sums[rows:]
    correction = (values - key_sums * decay) * beta
    overlap = jnp.sum(queries * keys_unit, axis=1, keepdims=True)
    readout = query_sums * decay + overlap * correction
    normed = readout * row_scale(readout) * head_gain[...]
    gated = (normed * (out_gate * jax.nn.sigmoid(out_gate))).astype(BF)
    attention = jnp.dot(gated, w_out[...], preferred_element_type=F32).astype(BF)
    piece = out.shape[2]
    for m in range(out.shape[0]):
        out[m] = attention[:, m * piece : (m + 1) * piece]


def residual_kernel(attention, hidden, gain, gained, residual):
    members, rows, piece = attention.shape
    total = hidden[...]
    for m in range(members):
        total = total + attention[m].astype(F32)
    residual[...] = total
    sent = (total * gain[...]).astype(BF)
    for d in range(gained.shape[0]):
        gained[d] = sent


def packed(tile, piece):
    if piece >= LANES:
        return [tile[:, c : c + LANES] for c in range(0, piece, LANES)]
    count = LANES // piece
    part = tile.shape[0] // count
    return [jnp.concatenate([tile[c * part : (c + 1) * part] for c in range(count)], axis=1)]


def unpacked(tile, rows, piece):
    if piece >= LANES:
        return jnp.concatenate(
            [tile[c * rows : (c + 1) * rows] for c in range(piece // LANES)], axis=1
        )
    return jnp.concatenate([tile[:, c : c + piece] for c in range(0, LANES, piece)], axis=0)


def tail_of(weight):
    part = 8
    lane = lax.broadcasted_iota(jnp.int32, (part, LANES), 1)
    tail = jnp.zeros((part, LANES), F32)
    for c in range(weight.shape[0] // part):
        at = weight[c * part : (c + 1) * part]
        high = at.astype(BF).astype(F32)
        tail = jnp.where(lane == c, high, tail)
        tail = jnp.where(lane == LANES // 2 + c, at - high, tail)
    return tail


def expert_kernel(width, every, hits, gain, own, other, out):
    devices, rows, piece = every.shape
    members = width // piece
    half = devices // members
    total_rows = half * rows
    span = 2 * MOE_FF
    experts = (own, other)
    gate_up = [jnp.zeros((total_rows, span), F32)] * 2
    routed = [jnp.zeros((total_rows, piece), F32)] * 2
    squares = jnp.zeros((total_rows, piece), F32)
    inverse = 1.0 / gain[...]
    last = own.shape[0] - 16
    routers = [ref[last:, :].astype(F32) for ref in experts]
    for m in range(members):
        columns = slice(m * piece, (m + 1) * piece)
        line, first = m * piece // span, m * piece % span
        x = jnp.concatenate([every[g * members + m] for g in range(half)], axis=0)
        wide = x.astype(F32)
        plain = wide * inverse[:, columns]
        squares = squares + plain * plain
        for i in range(2):
            gate_up[i] = gate_up[i] + jnp.dot(x, experts[i][columns, :], preferred_element_type=F32)
            routed[i] = routed[i] + wide * routers[i][line : line + 1, first : first + piece]
    scale = lax.rsqrt(jnp.sum(squares, axis=1, keepdims=True) * (1.0 / width) + EPS)
    weights, acts = [], []
    for i in range(2):
        logits = jnp.sum(routed[i], axis=1, keepdims=True) * scale
        weights.append(jnp.where(hits[:, i : i + 1] > 0.0, jnp.exp(logits), 0.0))
        both = gate_up[i] * scale
        gate = both[:, :MOE_FF]
        acts.append((gate * jax.nn.sigmoid(gate) * both[:, MOE_FF:]).astype(BF))
    summed = weights[0] + weights[1]
    tails = [tail_of(summed[g * rows : (g + 1) * rows]) for g in range(half)]
    for c in range(width // span):
        down = slice(width + c * MOE_FF, width + (c + 1) * MOE_FF)
        y = jnp.zeros((total_rows, span), F32)
        for i in range(2):
            y = y + jnp.dot(acts[i], experts[i][down, :], preferred_element_type=F32) * weights[i]
        for m in range(span // piece):
            for g in range(half):
                tile = y[g * rows : (g + 1) * rows, m * piece : (m + 1) * piece]
                out[g * members + c * span // piece + m] = jnp.concatenate(
                    packed(tile, piece) + [tails[g]], axis=0
                ).astype(BF)


def final_kernel(back, residual, out):
    devices, height, _ = back.shape
    rows, piece = residual.shape
    total = back[0].astype(F32)
    for d in range(1, devices):
        total = total + back[d].astype(F32)
    body = rows * piece // LANES
    numerator = unpacked(total[:body], rows, piece)
    tail = total[body:]
    tail = tail + pltpu.roll(tail, LANES // 2, 1)
    denominator = jnp.concatenate(
        [tail[:, c : c + 1] for c in range(rows // tail.shape[0])], axis=0
    )
    out[...] = (residual[...] + numerator / denominator).astype(BF)


def per_device(
    hidden,
    states,
    migration,
    routes,
    w_qkvz,
    w_ba,
    a_log,
    dt_bias,
    attn_gain,
    head_gain,
    w_out,
    moe_gain,
    w_router,
    w_gate_up,
    w_down,
):
    dp = ("x", "core")
    half = lax.axis_size("x")
    groups = half * lax.axis_size("core")
    members = lax.axis_size("expert")
    rows, width = hidden.shape
    depth = w_qkvz.shape[0]
    piece = width // members
    total_rows = routes.shape[0]
    leave_count = migration.shape[0] // groups
    plan = jnp.transpose(migration)
    shape = jax.ShapeDtypeStruct

    w_ba_t = jnp.transpose(w_ba)
    firsts = pl.pallas_call(
        functools.partial(first_kernel, groups, leave_count),
        out_shape=[pltpu.VMEM((depth, DK), BF)]
        + [pltpu.VMEM((rows * depth // LANES + DK, LANES), BF)] * (groups - 1)
        + [
            pltpu.VMEM((rows, DK, DV), F32),
            pltpu.VMEM(hidden.shape, BF),
            pltpu.VMEM(w_ba_t.shape, BF),
            pltpu.VMEM(hidden.shape, BF),
        ],
        in_specs=[HBM] * 6,
        out_specs=[VMEM] * (groups + 4),
        scratch_shapes=[
            pltpu.VMEM((1, width), F32),
            pltpu.SMEM(plan.shape, jnp.int32),
            pltpu.SemaphoreType.DMA,
            pltpu.SemaphoreType.DMA((5,)),
        ],
        compiler_params=PARAMS,
        cost_estimate=COST,
        name="first",
    )(*in_hbm(plan, states, hidden, w_qkvz, attn_gain.reshape(1, width), w_ba_t))
    held, hidden_near, w_ba_near, normed = firsts[groups:]
    other_qk = swap_with(firsts[0], "expert", 1)
    messages = [swap_with(firsts[i], dp, i) for i in range(1, groups)]
    operands = [head_gain.reshape(1, DV), moe_gain.reshape(1, width)]
    span = 2 * MOE_FF
    staged = pl.pallas_call(
        functools.partial(stage_kernel, groups),
        out_shape=[pltpu.VMEM(operand.shape, operand.dtype) for operand in operands]
        + [
            pltpu.VMEM((rows, piece), F32),
            pltpu.VMEM((1, piece), F32),
            pltpu.VMEM((total_rows // 2, LANES), F32),
            pltpu.VMEM((width + width // span * MOE_FF + 16, span), BF),
        ],
        in_specs=[VMEM] * 4 + [HBM] * (2 + len(operands)),
        out_specs=[VMEM] * (4 + len(operands)),
        scratch_shapes=[pltpu.SemaphoreType.DMA((1 + width // span + len(operands),))],
        compiler_params=PARAMS,
        cost_estimate=COST,
        name="stage",
    )(
        hidden_near,
        *in_hbm(moe_gain.reshape(1, width), jnp.transpose(routes), jnp.transpose(w_router)),
        *in_hbm(w_gate_up, w_down, *operands),
    )
    head_gain_near, moe_gain_near = staged[:-4]
    own_hidden, own_gain, hits, expert = staged[-4:]

    partials = pl.pallas_call(
        functools.partial(project_kernel, groups),
        out_shape=[pltpu.VMEM((rows, SENT), F32)] * groups,
        in_specs=[VMEM] * (3 + groups) + [ANY],
        out_specs=[VMEM] * groups,
        scratch_shapes=[pltpu.VMEM((total_rows, depth), BF)],
        compiler_params=PARAMS,
        cost_estimate=COST,
        name="project",
    )(normed, w_ba_near, w_qkvz, *messages[::-1], other_qk, own_gain)
    after = partials[0]
    partials = [partials[0]] + [swap_with(partials[i], dp, i) for i in range(1, groups)]
    split, mixing = pl.pallas_call(
        functools.partial(settle_kernel, groups, leave_count),
        out_shape=[pltpu.VMEM((rows * DK, 2 * DV), BF), pltpu.VMEM((2, LANES), F32)],
        in_specs=[HBM] + [SMEM] * 2 + [VMEM, ANY] + [VMEM] * (groups - 1),
        out_specs=[VMEM] * 2,
        scratch_shapes=[pltpu.SMEM(plan.shape, jnp.int32), pltpu.SemaphoreType.DMA],
        compiler_params=PARAMS,
        cost_estimate=COST,
        name="settle",
    )(*in_hbm(plan), a_log, dt_bias, held, after, *messages)

    attention, expert = pl.pallas_call(
        delta_kernel,
        out_shape=[
            pltpu.VMEM((members, rows, piece), BF),
            pltpu.VMEM(expert.shape, expert.dtype),
        ],
        in_specs=[VMEM] * 4 + [ANY] + [VMEM] * groups,
        out_specs=[VMEM, ANY],
        scratch_shapes=[pltpu.VMEM((4 * rows, rows * DK), BF)],
        input_output_aliases={4: 1},
        compiler_params=PARAMS,
        cost_estimate=COST,
        name="delta",
    )(mixing, head_gain_near, w_out, split, expert, *partials[::-1])
    other_expert = swap_with(expert, "core", 1)
    attention = lax.all_to_all(attention, "expert", split_axis=0, concat_axis=0, tiled=True)

    gained, residual = pl.pallas_call(
        residual_kernel,
        out_shape=[
            pltpu.VMEM((half * members, rows, piece), BF),
            pltpu.VMEM((rows, piece), F32),
        ],
        in_specs=[VMEM] * 3,
        out_specs=[VMEM] * 2,
        compiler_params=PARAMS,
        cost_estimate=COST,
        name="residual",
    )(attention, own_hidden, own_gain)
    every = lax.all_to_all(gained, ("x", "expert"), split_axis=0, concat_axis=0, tiled=True)

    height = rows * piece // LANES + 8
    sent = pl.pallas_call(
        functools.partial(expert_kernel, width),
        out_shape=pltpu.VMEM((half * members, height, LANES), BF),
        in_specs=[VMEM] * 5,
        out_specs=VMEM,
        compiler_params=PARAMS,
        cost_estimate=COST,
        name="experts",
    )(every, hits, moe_gain_near, expert, other_expert)
    back = lax.all_to_all(sent, ("x", "expert"), split_axis=0, concat_axis=0, tiled=True)
    return pl.pallas_call(
        final_kernel,
        out_shape=shape((rows, piece), BF),
        in_specs=[VMEM] * 2,
        out_specs=VMEM,
        compiler_params=PARAMS,
        cost_estimate=COST,
        name="finish",
    )(back, residual)


def solution(mesh):
    parts, groups, members = (mesh.shape[name] for name in ("parts", "dp", "expert"))
    devices = mesh.devices.reshape(parts, groups // 2, 2, members)
    fine = jax.sharding.Mesh(devices, ("parts", "x", "core", "expert"))
    placed = (
        P(("parts", "x", "core"), None),
        P(("parts", "x", "core"), "expert", None, None),
        P("parts", None),
        P("parts", None),
        P(("x", "core"), "expert"),
        P(("x", "core"), "expert"),
        P("expert"),
        P("expert"),
        P(),
        P(),
        P("expert", None),
        P(),
        P(None, ("x", "core", "expert")),
        P(("x", "core", "expert"), None, None),
        P(("x", "core", "expert"), None, None),
    )
    return jax.shard_map(
        per_device,
        mesh=fine,
        in_specs=placed,
        out_specs=P(("parts", "x", "core"), "expert"),
        check_vma=False,
    )
```

```python
import functools

import jax
import jax.numpy as jnp
from jax import lax
from jax.experimental import pallas as pl
from jax.experimental.pallas import tpu as pltpu
from jax.sharding import PartitionSpec as P

DK = 128
DV = 128
MOE_FF = 256
LANES = 128
SENT = 2 * DK + 2 * DV + LANES

EPS = 1e-06
BF = jnp.bfloat16
F32 = jnp.float32

VMEM = pl.BlockSpec(memory_space=pltpu.VMEM)
SMEM = pl.BlockSpec(memory_space=pltpu.SMEM)
HBM = pl.BlockSpec(memory_space=pltpu.HBM)
ANY = pl.BlockSpec(memory_space=pl.ANY)
COST = pl.CostEstimate(flops=0, bytes_accessed=8 * 1024 * 1024, transcendentals=0)
PARAMS = pltpu.CompilerParams(vmem_limit_bytes=24 * 1024 * 1024)


def in_hbm(*values):
    return [pltpu.with_memory_space_constraint(value, pltpu.HBM) for value in values]


def copy_all(pairs, sems):
    copies = [pltpu.make_async_copy(a, b, sems.at[i]) for i, (a, b) in enumerate(pairs)]
    for copy in copies:
        copy.start()
    return copies


def swap_with(value, axis, offset):
    pairs = [(source, source ^ offset) for source in range(lax.axis_size(axis))]
    return lax.ppermute(value, axis, pairs)


def row_scale(values):
    return lax.rsqrt(jnp.mean(values * values, axis=-1, keepdims=True) + EPS)


def unit_rows(values):
    return values * lax.rsqrt(jnp.sum(values * values, axis=-1, keepdims=True) + EPS)


def group_index():
    return lax.axis_index("x") * lax.axis_size("core") + lax.axis_index("core")


def first_kernel(groups, leave_count, migration, states, hidden, w_qkvz, *refs):
    gain, w_ba, own_qk, messages = refs[0], refs[1], refs[2], refs[3 : groups + 2]
    held, hidden_near, w_ba_near, normed, plan, gain_near, plan_sem, sems = refs[groups + 2 :]
    plan_copy = pltpu.make_async_copy(migration, plan, plan_sem)
    plan_copy.start()
    pairs = [
        (hidden, hidden_near),
        (states.at[:, 0], held),
        (w_qkvz.at[:, pl.ds(0, DK)], own_qk),
        (gain, gain_near),
        (w_ba, w_ba_near),
    ]
    copies = copy_all(pairs, sems)
    group = group_index()
    rows = hidden.shape[0]
    depth = w_qkvz.shape[0]
    tiles = depth // LANES
    copies[0].wait()
    wide = hidden_near[...].astype(F32)
    copies[3].wait()
    normed[...] = (wide * row_scale(wide) * gain_near[...]).astype(BF)
    for i in range(1, groups):
        for c in range(tiles):
            first = pl.multiple_of((group ^ i) * depth + c * LANES, LANES)
            messages[i - 1][c * rows : (c + 1) * rows, :] = normed[:, pl.ds(first, LANES)]
    plan_copy.wait()
    copies[1].wait()
    for i in range(1, groups):
        slot = 0
        for j in range(leave_count):
            at = group * leave_count + j
            slot = jnp.where(plan[2, at] == (group ^ i), plan[1, at], slot)
        messages[i - 1][tiles * rows :, :] = held[slot].astype(BF)
    for copy in copies[2:3] + copies[4:]:
        copy.wait()


def project_kernel(groups, normed, w_ba, w_qkvz, *refs):
    messages, outs, scaled = refs[: groups - 1][::-1], refs[groups + 1 : -1], refs[-1]
    other_qk = refs[groups - 1]
    group = group_index()
    depth = w_qkvz.shape[0]
    rows = normed.shape[0]
    for c in range(depth // LANES):
        columns = pl.ds(pl.multiple_of(group * depth + c * LANES, LANES), LANES)
        for i in range(groups):
            part = normed[:, columns] if i == 0 else messages[i - 1][c * rows : (c + 1) * rows, :]
            scaled[i * rows : (i + 1) * rows, c * LANES : (c + 1) * LANES] = part
    x = scaled[...]
    main = jnp.dot(x, w_qkvz[...], preferred_element_type=F32)
    other = jnp.dot(x, other_qk[...], preferred_element_type=F32)
    wide = x.astype(F32)
    lane = lax.broadcasted_iota(jnp.int32, (groups * rows, LANES), 1)
    mixes = jnp.zeros((groups * rows, LANES), F32)
    for j in range(2):
        total = jnp.sum(wide * w_ba[j : j + 1, :].astype(F32), axis=1, keepdims=True)
        mixes = jnp.where(lane == j, total, mixes)
    for i in range(groups):
        block = slice(i * rows, (i + 1) * rows)
        kind = outs[i].dtype
        outs[i][:, : DK + 2 * DV] = main[block].astype(kind)
        outs[i][:, DK + 2 * DV : 2 * DK + 2 * DV] = other[block].astype(kind)
        outs[i][:, 2 * DK + 2 * DV :] = mixes[block].astype(kind)


def stage_kernel(groups, hidden, gain, routes, router, w_gate_up, w_down, *refs):
    count = (len(refs) - 5) // 2
    sources, staged = refs[:count], refs[count : 2 * count]
    own_hidden, own_gain, hits, expert, sems = refs[-5:]
    width = hidden.shape[1]
    span = 2 * MOE_FF
    pairs = [(w_gate_up.at[0], expert.at[pl.ds(0, width)])]
    for c in range(width // span):
        pairs.append(
            (
                w_down.at[0, :, pl.ds(c * span, span)],
                expert.at[pl.ds(width + c * MOE_FF, MOE_FF)],
            )
        )
    copies = copy_all(list(zip(sources, staged)) + pairs, sems)
    line = lax.broadcasted_iota(jnp.int32, (16, span), 0)
    block = jnp.zeros((16, span), F32)
    for c in range(width // span):
        block = jnp.where(line == c, router[:, c * span : (c + 1) * span].astype(F32), block)
    expert[expert.shape[0] - 16 :, :] = block.astype(BF)
    group = group_index()
    core = lax.axis_index("core")
    member = lax.axis_index("expert")
    rows = hidden.shape[0]
    total_rows = groups * rows
    piece = own_hidden.shape[1]
    members = width // piece
    own, own_g = hidden[:, :piece], gain[:, :piece]
    for m in range(1, members):
        columns = slice(m * piece, (m + 1) * piece)
        own = jnp.where(member == m, hidden[:, columns], own)
        own_g = jnp.where(member == m, gain[:, columns], own_g)
    own_hidden[...] = own.astype(F32)
    own_gain[...] = own_g
    served = total_rows // 2
    row = lax.broadcasted_iota(jnp.int32, (served, total_rows), 0)
    lane = lax.broadcasted_iota(jnp.int32, (served, total_rows), 1)
    same = lane == (2 * (row // rows) + core) * rows + row % rows
    at = lax.broadcasted_iota(jnp.int32, hits.shape, 1)
    table = jnp.zeros(hits.shape, F32)
    for i in range(2):
        found = jnp.where(routes[...] == (group ^ i) * members + member, 1.0, 0.0)
        found = jnp.max(found, axis=0, keepdims=True)
        column = jnp.sum(jnp.where(same, found, 0.0), axis=1, keepdims=True)
        table = jnp.where(at == i, column, table)
    hits[...] = table
    for copy in copies:
        copy.wait()


def store_split(out, row, state):
    high = state.astype(BF)
    where = pl.ds(pl.multiple_of(row * DK, DK), DK)
    out[where, :DV] = high
    out[where, DV:] = (state - high.astype(F32)).astype(BF)


def settle_kernel(groups, leave_count, plan, a_log, dt_bias, states, after, *refs):
    messages, (split, mixing) = refs[:-2], refs[-2:]
    del after
    mixing[0:1, :] = jnp.exp(jnp.full((1, LANES), a_log[0], F32))
    mixing[1:2, :] = jnp.full((1, LANES), dt_bias[0], F32)
    group = group_index()
    for r in range(states.shape[0]):
        store_split(split, r, states[r])
    for i in range(groups):
        for j in range(leave_count):
            at = (group ^ i) * leave_count + j

            @pl.when(plan[2, at] == group)
            def _():
                if i == 0:
                    state = states[plan[1, at]]
                else:
                    arrival = messages[i - 1]
                    state = arrival[arrival.shape[0] - DK :, :].astype(F32)
                store_split(split, plan[3, at], state)


def delta_kernel(mixing, head_gain, w_out, split, expert, *refs):
    partials, (out, passed, blocks) = refs[:-3], refs[-3:]
    del expert, passed
    member = lax.axis_index("expert")
    rows = split.shape[0] // DK
    summed = partials[0][...].astype(F32)
    for partial in partials[1:]:
        summed = summed + partial[...].astype(F32)
    projected = summed.astype(BF).astype(F32)
    own_qk = projected[:, :DK]
    values = projected[:, DK : DK + DV]
    out_gate = projected[:, DK + DV : DK + 2 * DV]
    other = projected[:, DK + 2 * DV : 2 * DK + 2 * DV]
    write_mix = projected[:, 2 * DK + 2 * DV : 2 * DK + 2 * DV + 1]
    decay_mix = projected[:, 2 * DK + 2 * DV + 1 : 2 * DK + 2 * DV + 2]
    is_first = member % 2 == 0
    first = jnp.where(is_first, own_qk, other)
    second = jnp.where(is_first, other, own_qk)
    low_half = lax.broadcasted_iota(jnp.int32, (rows, DK), 1) < DK // 2
    queries = unit_rows(jnp.where(low_half, first, pltpu.roll(second, DK // 2, 1))) * DK ** (-0.5)
    keys_unit = unit_rows(jnp.where(low_half, pltpu.roll(first, DK // 2, 1), second))
    shifted = decay_mix + mixing[1:2, 0:1]
    soft = jnp.maximum(shifted, 0.0) + jnp.log1p(jnp.exp(-jnp.abs(shifted)))
    decay = jnp.exp(-mixing[0:1, 0:1] * soft)
    beta = jax.nn.sigmoid(write_mix)
    both = jnp.concatenate([keys_unit, queries], axis=0)
    high = both.astype(BF).astype(F32)
    both = jnp.concatenate([high, both - high], axis=0)
    row = lax.broadcasted_iota(jnp.int32, both.shape, 0) % rows
    for r in range(rows):
        blocks[:, r * DK : (r + 1) * DK] = jnp.where(row == r, both, 0.0).astype(BF)
    sums = jnp.dot(blocks[...], split[...], preferred_element_type=F32)
    sums = sums[:, :DV] + sums[:, DV:]
    sums = sums[: 2 * rows] + sums[2 * rows :]
    key_sums, query_sums = sums[:rows], sums[rows:]
    correction = (values - key_sums * decay) * beta
    overlap = jnp.sum(queries * keys_unit, axis=1, keepdims=True)
    readout = query_sums * decay + overlap * correction
    normed = readout * row_scale(readout) * head_gain[...]
    gated = (normed * (out_gate * jax.nn.sigmoid(out_gate))).astype(BF)
    attention = jnp.dot(gated, w_out[...], preferred_element_type=F32).astype(BF)
    piece = out.shape[2]
    for m in range(out.shape[0]):
        out[m] = attention[:, m * piece : (m + 1) * piece]


def residual_kernel(attention, hidden, gain, gained, residual):
    members, rows, piece = attention.shape
    total = hidden[...]
    for m in range(members):
        total = total + attention[m].astype(F32)
    residual[...] = total
    sent = (total * gain[...]).astype(BF)
    for d in range(gained.shape[0]):
        gained[d] = sent


def packed(tile, piece):
    if piece >= LANES:
        return [tile[:, c : c + LANES] for c in range(0, piece, LANES)]
    count = LANES // piece
    part = tile.shape[0] // count
    return [jnp.concatenate([tile[c * part : (c + 1) * part] for c in range(count)], axis=1)]


def unpacked(tile, rows, piece):
    if piece >= LANES:
        return jnp.concatenate(
            [tile[c * rows : (c + 1) * rows] for c in range(piece // LANES)], axis=1
        )
    return jnp.concatenate([tile[:, c : c + piece] for c in range(0, LANES, piece)], axis=0)


def tail_of(weight):
    part = 8
    lane = lax.broadcasted_iota(jnp.int32, (part, LANES), 1)
    tail = jnp.zeros((part, LANES), F32)
    for c in range(weight.shape[0] // part):
        at = weight[c * part : (c + 1) * part]
        high = at.astype(BF).astype(F32)
        tail = jnp.where(lane == c, high, tail)
        tail = jnp.where(lane == LANES // 2 + c, at - high, tail)
    return tail


def expert_kernel(width, every, hits, gain, own, other, out):
    devices, rows, piece = every.shape
    members = width // piece
    half = devices // members
    total_rows = half * rows
    span = 2 * MOE_FF
    experts = (own, other)
    gate_up = [jnp.zeros((total_rows, span), F32)] * 2
    routed = [jnp.zeros((total_rows, piece), F32)] * 2
    squares = jnp.zeros((total_rows, piece), F32)
    inverse = 1.0 / gain[...]
    last = own.shape[0] - 16
    routers = [ref[last:, :].astype(F32) for ref in experts]
    for m in range(members):
        columns = slice(m * piece, (m + 1) * piece)
        line, first = m * piece // span, m * piece % span
        x = jnp.concatenate([every[g * members + m] for g in range(half)], axis=0)
        wide = x.astype(F32)
        plain = wide * inverse[:, columns]
        squares = squares + plain * plain
        for i in range(2):
            gate_up[i] = gate_up[i] + jnp.dot(x, experts[i][columns, :], preferred_element_type=F32)
            routed[i] = routed[i] + wide * routers[i][line : line + 1, first : first + piece]
    scale = lax.rsqrt(jnp.sum(squares, axis=1, keepdims=True) * (1.0 / width) + EPS)
    weights, acts = [], []
    for i in range(2):
        logits = jnp.sum(routed[i], axis=1, keepdims=True) * scale
        weights.append(jnp.where(hits[:, i : i + 1] > 0.0, jnp.exp(logits), 0.0))
        both = gate_up[i] * scale
        gate = both[:, :MOE_FF]
        acts.append((gate * jax.nn.sigmoid(gate) * both[:, MOE_FF:]).astype(BF))
    summed = weights[0] + weights[1]
    tails = [tail_of(summed[g * rows : (g + 1) * rows]) for g in range(half)]
    for c in range(width // span):
        down = slice(width + c * MOE_FF, width + (c + 1) * MOE_FF)
        y = jnp.zeros((total_rows, span), F32)
        for i in range(2):
            y = y + jnp.dot(acts[i], experts[i][down, :], preferred_element_type=F32) * weights[i]
        for m in range(span // piece):
            for g in range(half):
                tile = y[g * rows : (g + 1) * rows, m * piece : (m + 1) * piece]
                out[g * members + c * span // piece + m] = jnp.concatenate(
                    packed(tile, piece) + [tails[g]], axis=0
                ).astype(BF)


def final_kernel(back, residual, out):
    devices, height, _ = back.shape
    rows, piece = residual.shape
    total = back[0].astype(F32)
    for d in range(1, devices):
        total = total + back[d].astype(F32)
    body = rows * piece // LANES
    numerator = unpacked(total[:body], rows, piece)
    tail = total[body:]
    tail = tail + pltpu.roll(tail, LANES // 2, 1)
    denominator = jnp.concatenate(
        [tail[:, c : c + 1] for c in range(rows // tail.shape[0])], axis=0
    )
    out[...] = (residual[...] + numerator / denominator).astype(BF)


def per_device(
    hidden,
    states,
    migration,
    routes,
    w_qkvz,
    w_ba,
    a_log,
    dt_bias,
    attn_gain,
    head_gain,
    w_out,
    moe_gain,
    w_router,
    w_gate_up,
    w_down,
):
    dp = ("x", "core")
    half = lax.axis_size("x")
    groups = half * lax.axis_size("core")
    members = lax.axis_size("expert")
    rows, width = hidden.shape
    depth = w_qkvz.shape[0]
    piece = width // members
    total_rows = routes.shape[0]
    leave_count = migration.shape[0] // groups
    plan = jnp.transpose(migration)
    shape = jax.ShapeDtypeStruct

    w_ba_t = jnp.transpose(w_ba)
    firsts = pl.pallas_call(
        functools.partial(first_kernel, groups, leave_count),
        out_shape=[pltpu.VMEM((depth, DK), BF)]
        + [pltpu.VMEM((rows * depth // LANES + DK, LANES), BF)] * (groups - 1)
        + [
            pltpu.VMEM((rows, DK, DV), F32),
            pltpu.VMEM(hidden.shape, BF),
            pltpu.VMEM(w_ba_t.shape, BF),
            pltpu.VMEM(hidden.shape, BF),
            pltpu.SMEM(plan.shape, jnp.int32),
        ],
        in_specs=[HBM] * 6,
        out_specs=[VMEM] * (groups + 4) + [SMEM],
        scratch_shapes=[
            pltpu.VMEM((1, width), F32),
            pltpu.SemaphoreType.DMA,
            pltpu.SemaphoreType.DMA((5,)),
        ],
        compiler_params=PARAMS,
        cost_estimate=COST,
        name="first",
    )(*in_hbm(plan, states, hidden, w_qkvz, attn_gain.reshape(1, width), w_ba_t))
    held, hidden_near, w_ba_near, normed, plan_near = firsts[groups:]
    other_qk = swap_with(firsts[0], "expert", 1)
    messages = [swap_with(firsts[i], dp, i) for i in range(1, groups)]
    operands = [head_gain.reshape(1, DV), moe_gain.reshape(1, width)]
    span = 2 * MOE_FF
    staged = pl.pallas_call(
        functools.partial(stage_kernel, groups),
        out_shape=[pltpu.VMEM(operand.shape, operand.dtype) for operand in operands]
        + [
            pltpu.VMEM((rows, piece), F32),
            pltpu.VMEM((1, piece), F32),
            pltpu.VMEM((total_rows // 2, LANES), F32),
            pltpu.VMEM((width + width // span * MOE_FF + 16, span), BF),
        ],
        in_specs=[VMEM] * 4 + [HBM] * (2 + len(operands)),
        out_specs=[VMEM] * (4 + len(operands)),
        scratch_shapes=[pltpu.SemaphoreType.DMA((1 + width // span + len(operands),))],
        compiler_params=PARAMS,
        cost_estimate=COST,
        name="stage",
    )(
        hidden_near,
        *in_hbm(moe_gain.reshape(1, width), jnp.transpose(routes), jnp.transpose(w_router)),
        *in_hbm(w_gate_up, w_down, *operands),
    )
    head_gain_near, moe_gain_near = staged[:-4]
    own_hidden, own_gain, hits, expert = staged[-4:]

    partials = pl.pallas_call(
        functools.partial(project_kernel, groups),
        out_shape=[pltpu.VMEM((rows, SENT), F32)] + [pltpu.VMEM((rows, SENT), BF)] * (groups - 1),
        in_specs=[VMEM] * (3 + groups) + [ANY],
        out_specs=[VMEM] * groups,
        scratch_shapes=[pltpu.VMEM((total_rows, depth), BF)],
        compiler_params=PARAMS,
        cost_estimate=COST,
        name="project",
    )(normed, w_ba_near, w_qkvz, *messages[::-1], other_qk, own_gain)
    after = partials[0]
    partials = [partials[0]] + [swap_with(partials[i], dp, i) for i in range(1, groups)]
    split, mixing = pl.pallas_call(
        functools.partial(settle_kernel, groups, leave_count),
        out_shape=[pltpu.VMEM((rows * DK, 2 * DV), BF), pltpu.VMEM((2, LANES), F32)],
        in_specs=[SMEM] * 3 + [VMEM, ANY] + [VMEM] * (groups - 1),
        out_specs=[VMEM] * 2,
        compiler_params=PARAMS,
        cost_estimate=COST,
        name="settle",
    )(plan_near, a_log, dt_bias, held, after, *messages)

    attention, expert = pl.pallas_call(
        delta_kernel,
        out_shape=[
            pltpu.VMEM((members, rows, piece), BF),
            pltpu.VMEM(expert.shape, expert.dtype),
        ],
        in_specs=[VMEM] * 4 + [ANY] + [VMEM] * groups,
        out_specs=[VMEM, ANY],
        scratch_shapes=[pltpu.VMEM((4 * rows, rows * DK), BF)],
        input_output_aliases={4: 1},
        compiler_params=PARAMS,
        cost_estimate=COST,
        name="delta",
    )(mixing, head_gain_near, w_out, split, expert, *partials[::-1])
    other_expert = swap_with(expert, "core", 1)
    attention = lax.all_to_all(attention, "expert", split_axis=0, concat_axis=0, tiled=True)

    gained, residual = pl.pallas_call(
        residual_kernel,
        out_shape=[
            pltpu.VMEM((half * members, rows, piece), BF),
            pltpu.VMEM((rows, piece), F32),
        ],
        in_specs=[VMEM] * 3,
        out_specs=[VMEM] * 2,
        compiler_params=PARAMS,
        cost_estimate=COST,
        name="residual",
    )(attention, own_hidden, own_gain)
    every = lax.all_to_all(gained, ("x", "expert"), split_axis=0, concat_axis=0, tiled=True)

    height = rows * piece // LANES + 8
    sent = pl.pallas_call(
        functools.partial(expert_kernel, width),
        out_shape=pltpu.VMEM((half * members, height, LANES), BF),
        in_specs=[VMEM] * 5,
        out_specs=VMEM,
        compiler_params=PARAMS,
        cost_estimate=COST,
        name="experts",
    )(every, hits, moe_gain_near, expert, other_expert)
    back = lax.all_to_all(sent, ("x", "expert"), split_axis=0, concat_axis=0, tiled=True)
    return pl.pallas_call(
        final_kernel,
        out_shape=shape((rows, piece), BF),
        in_specs=[VMEM] * 2,
        out_specs=VMEM,
        compiler_params=PARAMS,
        cost_estimate=COST,
        name="finish",
    )(back, residual)


def solution(mesh):
    parts, groups, members = (mesh.shape[name] for name in ("parts", "dp", "expert"))
    devices = mesh.devices.reshape(parts, groups // 2, 2, members)
    fine = jax.sharding.Mesh(devices, ("parts", "x", "core", "expert"))
    placed = (
        P(("parts", "x", "core"), None),
        P(("parts", "x", "core"), "expert", None, None),
        P("parts", None),
        P("parts", None),
        P(("x", "core"), "expert"),
        P(("x", "core"), "expert"),
        P("expert"),
        P("expert"),
        P(),
        P(),
        P("expert", None),
        P(),
        P(None, ("x", "core", "expert")),
        P(("x", "core", "expert"), None, None),
        P(("x", "core", "expert"), None, None),
    )
    return jax.shard_map(
        per_device,
        mesh=fine,
        in_specs=placed,
        out_specs=P(("parts", "x", "core"), "expert"),
        check_vma=False,
    )
```

```python
import functools

import jax
import jax.numpy as jnp
from jax import lax
from jax.experimental import pallas as pl
from jax.experimental.pallas import tpu as pltpu
from jax.sharding import PartitionSpec as P

DK = 128
DV = 128
MOE_FF = 256
LANES = 128
SENT = 2 * DK + 2 * DV + LANES

EPS = 1e-06
BF = jnp.bfloat16
F32 = jnp.float32

VMEM = pl.BlockSpec(memory_space=pltpu.VMEM)
SMEM = pl.BlockSpec(memory_space=pltpu.SMEM)
HBM = pl.BlockSpec(memory_space=pltpu.HBM)
ANY = pl.BlockSpec(memory_space=pl.ANY)
COST = pl.CostEstimate(flops=0, bytes_accessed=8 * 1024 * 1024, transcendentals=0)
PARAMS = pltpu.CompilerParams(vmem_limit_bytes=24 * 1024 * 1024)


def in_hbm(*values):
    return [pltpu.with_memory_space_constraint(value, pltpu.HBM) for value in values]


def copy_all(pairs, sems):
    copies = [pltpu.make_async_copy(a, b, sems.at[i]) for i, (a, b) in enumerate(pairs)]
    for copy in copies:
        copy.start()
    return copies


def swap_with(value, axis, offset):
    pairs = [(source, source ^ offset) for source in range(lax.axis_size(axis))]
    return lax.ppermute(value, axis, pairs)


def row_scale(values):
    return lax.rsqrt(jnp.mean(values * values, axis=-1, keepdims=True) + EPS)


def unit_rows(values):
    return values * lax.rsqrt(jnp.sum(values * values, axis=-1, keepdims=True) + EPS)


def group_index():
    return lax.axis_index("x") * lax.axis_size("core") + lax.axis_index("core")


def first_kernel(groups, leave_count, migration, states, hidden, w_qkvz, *refs):
    gain, w_ba, own_qk, messages = refs[0], refs[1], refs[2], refs[3 : groups + 2]
    held, hidden_near, w_ba_near, normed, plan, gain_near, plan_sem, sems = refs[groups + 2 :]
    plan_copy = pltpu.make_async_copy(migration, plan, plan_sem)
    plan_copy.start()
    pairs = [
        (hidden, hidden_near),
        (states.at[:, 0], held),
        (w_qkvz.at[:, pl.ds(0, DK)], own_qk),
        (gain, gain_near),
        (w_ba, w_ba_near),
    ]
    copies = copy_all(pairs, sems)
    group = group_index()
    rows = hidden.shape[0]
    depth = w_qkvz.shape[0]
    tiles = depth // LANES
    copies[0].wait()
    wide = hidden_near[...].astype(F32)
    copies[3].wait()
    normed[...] = (wide * row_scale(wide) * gain_near[...]).astype(BF)
    for i in range(1, groups):
        for c in range(tiles):
            first = pl.multiple_of((group ^ i) * depth + c * LANES, LANES)
            messages[i - 1][c * rows : (c + 1) * rows, :] = normed[:, pl.ds(first, LANES)]
    plan_copy.wait()
    copies[1].wait()
    for i in range(1, groups):
        slot = 0
        for j in range(leave_count):
            at = group * leave_count + j
            slot = jnp.where(plan[2, at] == (group ^ i), plan[1, at], slot)
        messages[i - 1][tiles * rows :, :] = held[slot].astype(BF)
    for copy in copies[2:3] + copies[4:]:
        copy.wait()


def project_kernel(groups, normed, w_ba, w_qkvz, *refs):
    messages, outs, scaled = refs[: groups - 1][::-1], refs[groups + 1 : -1], refs[-1]
    other_qk = refs[groups - 1]
    group = group_index()
    depth = w_qkvz.shape[0]
    rows = normed.shape[0]
    for c in range(depth // LANES):
        columns = pl.ds(pl.multiple_of(group * depth + c * LANES, LANES), LANES)
        for i in range(groups):
            part = normed[:, columns] if i == 0 else messages[i - 1][c * rows : (c + 1) * rows, :]
            scaled[i * rows : (i + 1) * rows, c * LANES : (c + 1) * LANES] = part
    x = scaled[...]
    main = jnp.dot(x, w_qkvz[...], preferred_element_type=F32)
    other = jnp.dot(x, other_qk[...], preferred_element_type=F32)
    wide = x.astype(F32)
    lane = lax.broadcasted_iota(jnp.int32, (groups * rows, LANES), 1)
    mixes = jnp.zeros((groups * rows, LANES), F32)
    for j in range(2):
        total = jnp.sum(wide * w_ba[j : j + 1, :].astype(F32), axis=1, keepdims=True)
        mixes = jnp.where(lane == j, total, mixes)
    for i in range(groups):
        block = slice(i * rows, (i + 1) * rows)
        kind = outs[i].dtype
        outs[i][:, : DK + 2 * DV] = main[block].astype(kind)
        outs[i][:, DK + 2 * DV : 2 * DK + 2 * DV] = other[block].astype(kind)
        outs[i][:, 2 * DK + 2 * DV :] = mixes[block].astype(kind)


def stage_kernel(groups, hidden, gain, routes, router, w_gate_up, w_down, *refs):
    count = (len(refs) - 5) // 2
    sources, staged = refs[:count], refs[count : 2 * count]
    own_hidden, own_gain, hits, expert, sems = refs[-5:]
    width = hidden.shape[1]
    span = 2 * MOE_FF
    pairs = [(w_gate_up.at[0], expert.at[pl.ds(0, width)])]
    for c in range(width // span):
        pairs.append(
            (
                w_down.at[0, :, pl.ds(c * span, span)],
                expert.at[pl.ds(width + c * MOE_FF, MOE_FF)],
            )
        )
    copies = copy_all(list(zip(sources, staged)) + pairs, sems)
    line = lax.broadcasted_iota(jnp.int32, (16, span), 0)
    block = jnp.zeros((16, span), F32)
    for c in range(width // span):
        block = jnp.where(line == c, router[:, c * span : (c + 1) * span].astype(F32), block)
    expert[expert.shape[0] - 16 :, :] = block.astype(BF)
    group = group_index()
    core = lax.axis_index("core")
    member = lax.axis_index("expert")
    rows = hidden.shape[0]
    total_rows = groups * rows
    piece = own_hidden.shape[1]
    members = width // piece
    own, own_g = hidden[:, :piece], gain[:, :piece]
    for m in range(1, members):
        columns = slice(m * piece, (m + 1) * piece)
        own = jnp.where(member == m, hidden[:, columns], own)
        own_g = jnp.where(member == m, gain[:, columns], own_g)
    own_hidden[...] = own.astype(F32)
    own_gain[...] = own_g
    served = total_rows // 2
    row = lax.broadcasted_iota(jnp.int32, (served, total_rows), 0)
    lane = lax.broadcasted_iota(jnp.int32, (served, total_rows), 1)
    same = lane == (2 * (row // rows) + core) * rows + row % rows
    at = lax.broadcasted_iota(jnp.int32, hits.shape, 1)
    table = jnp.zeros(hits.shape, F32)
    for i in range(2):
        found = jnp.where(routes[...] == (group ^ i) * members + member, 1.0, 0.0)
        found = jnp.max(found, axis=0, keepdims=True)
        column = jnp.sum(jnp.where(same, found, 0.0), axis=1, keepdims=True)
        table = jnp.where(at == i, column, table)
    hits[...] = table
    for copy in copies:
        copy.wait()


def store_split(out, row, state):
    high = state.astype(BF)
    where = pl.ds(pl.multiple_of(row * DK, DK), DK)
    out[where, :DV] = high
    out[where, DV:] = (state - high.astype(F32)).astype(BF)


def settle_kernel(groups, leave_count, plan, a_log, dt_bias, states, after, *refs):
    messages, (split, mixing) = refs[:-2], refs[-2:]
    del after
    mixing[0:1, :] = jnp.exp(jnp.full((1, LANES), a_log[0], F32))
    mixing[1:2, :] = jnp.full((1, LANES), dt_bias[0], F32)
    group = group_index()
    for r in range(states.shape[0]):
        store_split(split, r, states[r])
    for i in range(groups):
        for j in range(leave_count):
            at = (group ^ i) * leave_count + j

            @pl.when(plan[2, at] == group)
            def _():
                if i == 0:
                    state = states[plan[1, at]]
                else:
                    arrival = messages[i - 1]
                    state = arrival[arrival.shape[0] - DK :, :].astype(F32)
                store_split(split, plan[3, at], state)


def delta_kernel(mixing, head_gain, w_out, split, expert, *refs):
    partials, (out, passed, blocks) = refs[:-3], refs[-3:]
    del expert, passed
    member = lax.axis_index("expert")
    rows = split.shape[0] // DK
    summed = partials[0][...].astype(F32)
    for partial in partials[1:]:
        summed = summed + partial[...].astype(F32)
    projected = summed.astype(BF).astype(F32)
    own_qk = projected[:, :DK]
    values = projected[:, DK : DK + DV]
    out_gate = projected[:, DK + DV : DK + 2 * DV]
    other = projected[:, DK + 2 * DV : 2 * DK + 2 * DV]
    write_mix = projected[:, 2 * DK + 2 * DV : 2 * DK + 2 * DV + 1]
    decay_mix = projected[:, 2 * DK + 2 * DV + 1 : 2 * DK + 2 * DV + 2]
    is_first = member % 2 == 0
    first = jnp.where(is_first, own_qk, other)
    second = jnp.where(is_first, other, own_qk)
    low_half = lax.broadcasted_iota(jnp.int32, (rows, DK), 1) < DK // 2
    queries = unit_rows(jnp.where(low_half, first, pltpu.roll(second, DK // 2, 1))) * DK ** (-0.5)
    keys_unit = unit_rows(jnp.where(low_half, pltpu.roll(first, DK // 2, 1), second))
    shifted = decay_mix + mixing[1:2, 0:1]
    soft = jnp.maximum(shifted, 0.0) + jnp.log1p(jnp.exp(-jnp.abs(shifted)))
    decay = jnp.exp(-mixing[0:1, 0:1] * soft)
    beta = jax.nn.sigmoid(write_mix)
    both = jnp.concatenate([keys_unit, queries], axis=0)
    high = both.astype(BF).astype(F32)
    both = jnp.concatenate([high, both - high], axis=0)
    row = lax.broadcasted_iota(jnp.int32, both.shape, 0) % rows
    for r in range(rows):
        blocks[:, r * DK : (r + 1) * DK] = jnp.where(row == r, both, 0.0).astype(BF)
    sums = jnp.dot(blocks[...], split[...], preferred_element_type=F32)
    sums = sums[:, :DV] + sums[:, DV:]
    sums = sums[: 2 * rows] + sums[2 * rows :]
    key_sums, query_sums = sums[:rows], sums[rows:]
    correction = (values - key_sums * decay) * beta
    overlap = jnp.sum(queries * keys_unit, axis=1, keepdims=True)
    readout = query_sums * decay + overlap * correction
    normed = readout * row_scale(readout) * head_gain[...]
    gated = (normed * (out_gate * jax.nn.sigmoid(out_gate))).astype(BF)
    attention = jnp.dot(gated, w_out[...], preferred_element_type=F32).astype(BF)
    piece = out.shape[2]
    for m in range(out.shape[0]):
        out[m] = attention[:, m * piece : (m + 1) * piece]


def residual_kernel(attention, hidden, gain, gained, residual):
    members, rows, piece = attention.shape
    total = hidden[...]
    for m in range(members):
        total = total + attention[m].astype(F32)
    residual[...] = total
    sent = (total * gain[...]).astype(BF)
    for d in range(gained.shape[0]):
        gained[d] = sent


def packed(tile, piece):
    if piece >= LANES:
        return [tile[:, c : c + LANES] for c in range(0, piece, LANES)]
    count = LANES // piece
    part = tile.shape[0] // count
    return [jnp.concatenate([tile[c * part : (c + 1) * part] for c in range(count)], axis=1)]


def unpacked(tile, rows, piece):
    if piece >= LANES:
        return jnp.concatenate(
            [tile[c * rows : (c + 1) * rows] for c in range(piece // LANES)], axis=1
        )
    return jnp.concatenate([tile[:, c : c + piece] for c in range(0, LANES, piece)], axis=0)


def tail_of(weight):
    part = 8
    lane = lax.broadcasted_iota(jnp.int32, (part, LANES), 1)
    tail = jnp.zeros((part, LANES), F32)
    for c in range(weight.shape[0] // part):
        at = weight[c * part : (c + 1) * part]
        high = at.astype(BF).astype(F32)
        tail = jnp.where(lane == c, high, tail)
        tail = jnp.where(lane == LANES // 2 + c, at - high, tail)
    return tail


def expert_kernel(width, every, hits, gain, own, other, out):
    devices, rows, piece = every.shape
    members = width // piece
    half = devices // members
    total_rows = half * rows
    span = 2 * MOE_FF
    experts = (own, other)
    gate_up = [jnp.zeros((total_rows, span), F32)] * 2
    routed = [jnp.zeros((total_rows, piece), F32)] * 2
    squares = jnp.zeros((total_rows, piece), F32)
    inverse = 1.0 / gain[...]
    last = own.shape[0] - 16
    routers = [ref[last:, :].astype(F32) for ref in experts]
    for m in range(members):
        columns = slice(m * piece, (m + 1) * piece)
        line, first = m * piece // span, m * piece % span
        x = jnp.concatenate([every[g * members + m] for g in range(half)], axis=0)
        wide = x.astype(F32)
        plain = wide * inverse[:, columns]
        squares = squares + plain * plain
        for i in range(2):
            gate_up[i] = gate_up[i] + jnp.dot(x, experts[i][columns, :], preferred_element_type=F32)
            routed[i] = routed[i] + wide * routers[i][line : line + 1, first : first + piece]
    scale = lax.rsqrt(jnp.sum(squares, axis=1, keepdims=True) * (1.0 / width) + EPS)
    weights, acts = [], []
    for i in range(2):
        logits = jnp.sum(routed[i], axis=1, keepdims=True) * scale
        weights.append(jnp.where(hits[:, i : i + 1] > 0.0, jnp.exp(logits), 0.0))
        both = gate_up[i] * scale
        gate = both[:, :MOE_FF]
        acts.append((gate * jax.nn.sigmoid(gate) * both[:, MOE_FF:]).astype(BF))
    summed = weights[0] + weights[1]
    tails = [tail_of(summed[g * rows : (g + 1) * rows]) for g in range(half)]
    for c in range(width // span):
        down = slice(width + c * MOE_FF, width + (c + 1) * MOE_FF)
        y = jnp.zeros((total_rows, span), F32)
        for i in range(2):
            y = y + jnp.dot(acts[i], experts[i][down, :], preferred_element_type=F32) * weights[i]
        for m in range(span // piece):
            for g in range(half):
                tile = y[g * rows : (g + 1) * rows, m * piece : (m + 1) * piece]
                out[g * members + c * span // piece + m] = jnp.concatenate(
                    packed(tile, piece) + [tails[g]], axis=0
                ).astype(BF)


def final_kernel(back, residual, out):
    devices, height, _ = back.shape
    rows, piece = residual.shape
    total = back[0].astype(F32)
    for d in range(1, devices):
        total = total + back[d].astype(F32)
    body = rows * piece // LANES
    numerator = unpacked(total[:body], rows, piece)
    tail = total[body:]
    tail = tail + pltpu.roll(tail, LANES // 2, 1)
    denominator = jnp.concatenate(
        [tail[:, c : c + 1] for c in range(rows // tail.shape[0])], axis=0
    )
    out[...] = (residual[...] + numerator / denominator).astype(BF)


def per_device(
    hidden,
    states,
    migration,
    routes,
    w_qkvz,
    w_ba,
    a_log,
    dt_bias,
    attn_gain,
    head_gain,
    w_out,
    moe_gain,
    w_router,
    w_gate_up,
    w_down,
):
    dp = ("x", "core")
    half = lax.axis_size("x")
    groups = half * lax.axis_size("core")
    members = lax.axis_size("expert")
    rows, width = hidden.shape
    depth = w_qkvz.shape[0]
    piece = width // members
    total_rows = routes.shape[0]
    leave_count = migration.shape[0] // groups
    plan = jnp.transpose(migration)
    shape = jax.ShapeDtypeStruct

    w_ba_t = jnp.transpose(w_ba)
    firsts = pl.pallas_call(
        functools.partial(first_kernel, groups, leave_count),
        out_shape=[pltpu.VMEM((depth, DK), BF)]
        + [pltpu.VMEM((rows * depth // LANES + DK, LANES), BF)] * (groups - 1)
        + [
            pltpu.VMEM((rows, DK, DV), F32),
            pltpu.VMEM(hidden.shape, BF),
            pltpu.VMEM(w_ba_t.shape, BF),
            pltpu.VMEM(hidden.shape, BF),
            pltpu.SMEM(plan.shape, jnp.int32),
        ],
        in_specs=[HBM] * 6,
        out_specs=[VMEM] * (groups + 4) + [SMEM],
        scratch_shapes=[
            pltpu.VMEM((1, width), F32),
            pltpu.SemaphoreType.DMA,
            pltpu.SemaphoreType.DMA((5,)),
        ],
        compiler_params=PARAMS,
        cost_estimate=COST,
        name="first",
    )(*in_hbm(plan, states, hidden, w_qkvz, attn_gain.reshape(1, width), w_ba_t))
    held, hidden_near, w_ba_near, normed, plan_near = firsts[groups:]
    other_qk = swap_with(firsts[0], "expert", 1)
    messages = [swap_with(firsts[i], dp, i) for i in range(1, groups)]
    operands = [head_gain.reshape(1, DV), moe_gain.reshape(1, width)]
    span = 2 * MOE_FF
    staged = pl.pallas_call(
        functools.partial(stage_kernel, groups),
        out_shape=[pltpu.VMEM(operand.shape, operand.dtype) for operand in operands]
        + [
            pltpu.VMEM((rows, piece), F32),
            pltpu.VMEM((1, piece), F32),
            pltpu.VMEM((total_rows // 2, LANES), F32),
            pltpu.VMEM((width + width // span * MOE_FF + 16, span), BF),
        ],
        in_specs=[VMEM] * 4 + [HBM] * (2 + len(operands)),
        out_specs=[VMEM] * (4 + len(operands)),
        scratch_shapes=[pltpu.SemaphoreType.DMA((1 + width // span + len(operands),))],
        compiler_params=PARAMS,
        cost_estimate=COST,
        name="stage",
    )(
        hidden_near,
        *in_hbm(moe_gain.reshape(1, width), jnp.transpose(routes), jnp.transpose(w_router)),
        *in_hbm(w_gate_up, w_down, *operands),
    )
    head_gain_near, moe_gain_near = staged[:-4]
    own_hidden, own_gain, hits, expert = staged[-4:]

    partials = pl.pallas_call(
        functools.partial(project_kernel, groups),
        out_shape=[pltpu.VMEM((rows, SENT), F32)] + [pltpu.VMEM((rows, SENT), BF)] * (groups - 1),
        in_specs=[VMEM] * (3 + groups) + [ANY],
        out_specs=[VMEM] * groups,
        scratch_shapes=[pltpu.VMEM((total_rows, depth), BF)],
        compiler_params=PARAMS,
        cost_estimate=COST,
        name="project",
    )(normed, w_ba_near, w_qkvz, *messages[::-1], other_qk, own_gain)
    after = partials[0]
    partials = [partials[0]] + [swap_with(partials[i], dp, i) for i in range(1, groups)]
    split, mixing = pl.pallas_call(
        functools.partial(settle_kernel, groups, leave_count),
        out_shape=[pltpu.VMEM((rows * DK, 2 * DV), BF), pltpu.VMEM((2, LANES), F32)],
        in_specs=[SMEM] * 3 + [VMEM, ANY] + [VMEM] * (groups - 1),
        out_specs=[VMEM] * 2,
        compiler_params=PARAMS,
        cost_estimate=COST,
        name="settle",
    )(plan_near, a_log, dt_bias, held, after, *messages)

    attention, expert = pl.pallas_call(
        delta_kernel,
        out_shape=[
            pltpu.VMEM((members, rows, piece), BF),
            pltpu.VMEM(expert.shape, expert.dtype),
        ],
        in_specs=[VMEM] * 4 + [ANY] + [VMEM] * groups,
        out_specs=[VMEM, ANY],
        scratch_shapes=[pltpu.VMEM((4 * rows, rows * DK), BF)],
        input_output_aliases={4: 1},
        compiler_params=PARAMS,
        cost_estimate=COST,
        name="delta",
    )(mixing, head_gain_near, w_out, split, expert, *partials)
    other_expert = swap_with(expert, "core", 1)
    attention = lax.all_to_all(attention, "expert", split_axis=0, concat_axis=0, tiled=True)

    gained, residual = pl.pallas_call(
        residual_kernel,
        out_shape=[
            pltpu.VMEM((half * members, rows, piece), BF),
            pltpu.VMEM((rows, piece), F32),
        ],
        in_specs=[VMEM] * 3,
        out_specs=[VMEM] * 2,
        compiler_params=PARAMS,
        cost_estimate=COST,
        name="residual",
    )(attention, own_hidden, own_gain)
    every = lax.all_to_all(gained, ("x", "expert"), split_axis=0, concat_axis=0, tiled=True)

    height = rows * piece // LANES + 8
    sent = pl.pallas_call(
        functools.partial(expert_kernel, width),
        out_shape=pltpu.VMEM((half * members, height, LANES), BF),
        in_specs=[VMEM] * 5,
        out_specs=VMEM,
        compiler_params=PARAMS,
        cost_estimate=COST,
        name="experts",
    )(every, hits, moe_gain_near, expert, other_expert)
    back = lax.all_to_all(sent, ("x", "expert"), split_axis=0, concat_axis=0, tiled=True)
    return pl.pallas_call(
        final_kernel,
        out_shape=shape((rows, piece), BF),
        in_specs=[VMEM] * 2,
        out_specs=VMEM,
        compiler_params=PARAMS,
        cost_estimate=COST,
        name="finish",
    )(back, residual)


def solution(mesh):
    parts, groups, members = (mesh.shape[name] for name in ("parts", "dp", "expert"))
    devices = mesh.devices.reshape(parts, groups // 2, 2, members)
    fine = jax.sharding.Mesh(devices, ("parts", "x", "core", "expert"))
    placed = (
        P(("parts", "x", "core"), None),
        P(("parts", "x", "core"), "expert", None, None),
        P("parts", None),
        P("parts", None),
        P(("x", "core"), "expert"),
        P(("x", "core"), "expert"),
        P("expert"),
        P("expert"),
        P(),
        P(),
        P("expert", None),
        P(),
        P(None, ("x", "core", "expert")),
        P(("x", "core", "expert"), None, None),
        P(("x", "core", "expert"), None, None),
    )
    return jax.shard_map(
        per_device,
        mesh=fine,
        in_specs=placed,
        out_specs=P(("parts", "x", "core"), "expert"),
        check_vma=False,
    )
```
